32 devices in a mesh: dp: 2 (over y), ctx: 16 (over z, x, core).
Axes of the slice: x: 2, y: 2, z: 4, core: 2. Of those that a mesh axis runs over, the one named last changes fastest.
Arguments:
- queries: bfloat16 [2, 2048, 1024], P('dp', 'ctx'), may hold values from -6 to 6
- keys: bfloat16 [2, 2048, 1024], P('dp', 'ctx'), may hold values from -6 to 6
- values: bfloat16 [2, 2048, 1024], P('dp', 'ctx'), may hold values from -6 to 6
- rel_bias: float32 [16, 769], replicated, may hold values from -8 to 8
- grad_out: bfloat16 [2, 2048, 1024], P('dp', 'ctx'), may hold values from -6 to 6
Outputs:
- attended: bfloat16 [2, 2048, 1024], P('dp', 'ctx')
- grad_queries: bfloat16 [2, 2048, 1024], P('dp', 'ctx')
- grad_keys: bfloat16 [2, 2048, 1024], P('dp', 'ctx')
- grad_values: bfloat16 [2, 2048, 1024], P('dp', 'ctx')
- grad_bias: float32 [16, 769], replicated
The draws below stay inside these ranges and needn't reach their ends.
All inputs are finite; a program needn't handle non-finite values.
Results may differ from the reference program's by a relative error of at most 0.024.
Values may be sent and summed in bfloat16 or wider, within the bound.
A program may use at most 128 MiB of HBM per device.

```python
import math
import jax
import jax.numpy as jnp
from jax import lax

HEADS = 16
HEAD = 64
FR_DEV = 128
NB = 3
CONTEXT = 384
LENGTH = 2048
RECS = 2
WIDTH = 1024
N_CTX = 16


def draw_together(key):
    shape = (RECS, LENGTH, HEADS * HEAD)
    base = jax.random.fold_in(key, 11)
    query_key, keyed_key = jax.random.split(base, 2)
    query_draw = jnp.clip(jax.random.normal(query_key, shape, jnp.float32), -6.0, 6.0)
    keyed_draw = jnp.clip(jax.random.normal(keyed_key, shape, jnp.float32), -6.0, 6.0)
    return (query_draw, keyed_draw)


def draw_queries(key, part):
    return draw_together(key)[0].astype(jnp.bfloat16)


def draw_keys(key, part):
    return draw_together(key)[1].astype(jnp.bfloat16)


def shard_levels(stream_key, extent, pieces, low, largest):
    def one(dim, shards_of):
        heights = jax.random.uniform(jax.random.fold_in(jax.random.fold_in(stream_key, 6), dim), (shards_of,), jnp.float32, low / len(pieces), largest / len(pieces))
        return jnp.repeat(jnp.exp(heights), extent[dim] // shards_of).reshape((-1,) + (1,) * (len(extent) - dim - 1))

    loudness = one(*pieces[0])
    for cut in pieces[1:]:
        loudness = loudness * one(*cut)
    return loudness


def gaussian(key, extent, spread, reach, cuts=(), kind=jnp.bfloat16):
    values = jax.random.normal(key, extent, jnp.float32) * spread
    if len(cuts) > 0:
        values = shard_levels(key, extent, cuts, -0.22, 0.18) * values
    return jnp.clip(values, min=-reach, max=reach).astype(kind)


def setup_inputs(seed: int = 0) -> dict:
    splits = jax.random.split(jax.random.key(seed), 6)
    return {
        "queries": draw_queries(jax.random.fold_in(splits[5], 71), 0),
        "keys": draw_keys(jax.random.fold_in(splits[5], 71), 0),
        "values": gaussian(splits[2], (RECS, LENGTH, WIDTH), 1.0, 6.0, ((0, 2), (1, 16))),
        "rel_bias": gaussian(splits[3], (HEADS, 2 * CONTEXT + 1), 2.0, 8.0, (), jnp.float32),
        "grad_out": gaussian(splits[4], (RECS, LENGTH, WIDTH), 1.0, 6.0, ((0, 2), (1, 16))),
    }


excluded = -1e+30

def reference(queries, keys, values, rel_bias, grad_out):
    recs, length, width = queries.shape
    frames = FR_DEV
    blocks = N_CTX
    context = NB * frames
    span = (2 * NB + 1) * frames
    score_scale = 1.0 / math.sqrt(HEAD)
    shaped = (recs, blocks, frames, HEADS, HEAD)
    query_blocks = queries.reshape(shaped)
    grad_blocks = grad_out.reshape(shaped)
    padding = ((0, 0), (NB, NB), (0, 0), (0, 0), (0, 0))
    key_padded = jnp.pad(keys.reshape(shaped), padding)
    value_padded = jnp.pad(values.reshape(shaped), padding)
    row_index = jnp.arange(frames, dtype=jnp.int32)[:, None]
    col_index = jnp.arange(span, dtype=jnp.int32)[None, :]
    table_index = row_index - col_index + 2 * context
    inside = (table_index >= 0) & (table_index <= 2 * context)
    clipped = jnp.clip(table_index, 0, 2 * context)
    bias_table = rel_bias[:, clipped]

    def one_block(carry, block):
        key_accum, value_accum, bias_accum = carry
        query_now = lax.dynamic_index_in_dim(query_blocks, block, 1, keepdims=False).astype(jnp.float32)
        grad_now = lax.dynamic_index_in_dim(grad_blocks, block, 1, keepdims=False).astype(jnp.float32)
        key_window = lax.dynamic_slice_in_dim(key_padded, block, 2 * NB + 1, 1).reshape(recs, span, HEADS, HEAD).astype(jnp.float32)
        value_window = lax.dynamic_slice_in_dim(value_padded, block, 2 * NB + 1, 1).reshape(recs, span, HEADS, HEAD).astype(jnp.float32)
        key_place = (block - NB) * frames + col_index
        live = inside & (key_place >= 0) & (key_place < length)
        scores = jnp.einsum('rahe,rwhe->rhaw', query_now, key_window) * score_scale + bias_table[None]
        scores = jnp.where(live[None, None], scores, excluded)
        top = lax.optimization_barrier(jnp.max(scores, axis=-1))
        total = lax.optimization_barrier(jnp.sum(jnp.exp(scores - top[..., None]), axis=-1))
        log_norm = top + jnp.log(total)
        probs = jnp.exp(scores - log_norm[..., None])
        weights = lax.optimization_barrier(probs.astype(jnp.bfloat16)).astype(jnp.float32)
        output = jnp.einsum('rhaw,rwhe->rahe', weights, value_window)
        attended_now = output.astype(jnp.bfloat16)
        attended_wide = lax.optimization_barrier(attended_now).astype(jnp.float32)
        delta = jnp.einsum('rahe,rahe->rha', grad_now, attended_wide)
        dprob = jnp.einsum('rahe,rwhe->rhaw', grad_now, value_window)
        dscore = probs * (dprob - delta[..., None])
        dscore_low = lax.optimization_barrier(dscore.astype(jnp.bfloat16)).astype(jnp.float32)
        grad_query_now = (jnp.einsum('rhaw,rwhe->rahe', dscore_low, key_window) * score_scale).astype(jnp.bfloat16)
        key_terms = jnp.einsum('rhaw,rahe->rwhe', dscore_low, query_now) * score_scale
        value_terms = jnp.einsum('rhaw,rahe->rwhe', weights, grad_now)
        key_terms = lax.optimization_barrier(key_terms.astype(jnp.bfloat16)).astype(jnp.float32)
        value_terms = lax.optimization_barrier(value_terms.astype(jnp.bfloat16)).astype(jnp.float32)
        start = block * frames
        key_accum = lax.dynamic_update_slice_in_dim(key_accum, lax.dynamic_slice_in_dim(key_accum, start, span, 1) + key_terms, start, 1)
        value_accum = lax.dynamic_update_slice_in_dim(value_accum, lax.dynamic_slice_in_dim(value_accum, start, span, 1) + value_terms, start, 1)
        flat_terms = lax.optimization_barrier(jnp.sum(dscore, axis=0)).transpose(1, 2, 0).reshape(frames * span, HEADS)
        bias_accum = bias_accum + jax.ops.segment_sum(flat_terms, clipped.reshape(-1), num_segments=2 * context + 1)
        return ((key_accum, value_accum, bias_accum), (attended_now, grad_query_now))
    padded_rows = (blocks + 2 * NB) * frames
    start_carry = (jnp.zeros((recs, padded_rows, HEADS, HEAD), jnp.float32), jnp.zeros((recs, padded_rows, HEADS, HEAD), jnp.float32), jnp.zeros((2 * context + 1, HEADS), jnp.float32))
    final, stacked = lax.scan(one_block, start_carry, jnp.arange(blocks, dtype=jnp.int32))
    key_accum, value_accum, bias_accum = final
    attended = stacked[0].transpose(1, 0, 2, 3, 4).reshape(recs, length, width)
    grad_queries = stacked[1].transpose(1, 0, 2, 3, 4).reshape(recs, length, width)
    grad_keys = key_accum[:, context:context + length].astype(jnp.bfloat16).reshape(recs, length, width)
    grad_values = value_accum[:, context:context + length].astype(jnp.bfloat16).reshape(recs, length, width)
    grad_bias = bias_accum.T
    return (attended, grad_queries, grad_keys, grad_values, grad_bias)
```

```python
import functools
import math

import jax
import jax.numpy as jnp
from jax import lax
from jax.experimental import pallas as pl
from jax.experimental.pallas import tpu as pltpu
from jax.sharding import PartitionSpec as P

HEADS = 16
HEAD = 64
NB = 3
GROUP = 4
PAIRS = HEADS // GROUP // 2
LANES = 2 * HEAD
EXCLUDED = -1e30
MESH = pl.DeviceIdType.MESH
Q, K, V, G = 0, 1, 2, 3
NT = (((1,), (1,)), ((), ()))
TN = (((0,), (0,)), ((), ()))


def dot(a, b, dims=(((1,), (0,)), ((), ()))):
    return lax.dot_general(a, b, dims, preferred_element_type=jnp.float32)


def kernel(
    n_dp, n_groups, frames,
    q_hbm, k_hbm, v_hbm, g_hbm, rev_ref,
    att_out, gq_out, gk_out, gv_out, bias_out,
    qbuf, gbuf, kbuf, vbuf, bias_tab, bias_acc, gk_acc, gv_acc,
    halo_out, halo_in, ostage, b1buf, b2buf, sum_buf,
    loc_sem, a_send, a_recv, h_send, h_recv, g_send, g_recv,
    o_send, o_recv, o_loc, b1_send, b1_recv, b2_send, b2_recv,
):
    span = (2 * NB + 1) * frames
    ctxw = NB * frames
    own = GROUP * frames
    total_rows = own + 2 * ctxw
    score_scale = 1.0 / math.sqrt(HEAD)
    dp = lax.axis_index("dp")
    ctx = lax.axis_index("ctx")
    g = lax.div(ctx, GROUP)
    i = lax.rem(ctx, GROUP)
    n_peer = n_dp * n_groups
    slot = dp * n_groups + g
    has_lo = g > 0
    has_hi = g < n_groups - 1
    srcs = (q_hbm, k_hbm, v_hbm, g_hbm)
    outs = (att_out, gq_out, gk_out, gv_out)
    accs = (gk_acc, gv_acc)

    def group_dev(j):
        return {"dp": dp, "ctx": g * GROUP + j}

    def side_dev(direction):
        return {"dp": dp, "ctx": ctx + (GROUP if direction else -GROUP)}

    def peer_dev(s):
        return {"dp": lax.div(s, n_groups), "ctx": lax.rem(s, n_groups) * GROUP + i}

    def lanes(j, p):
        return pl.ds(pl.multiple_of((j * PAIRS + p) * LANES, LANES), LANES)

    def rows_of(arr, p, j):
        if arr in (K, V):
            start = pl.multiple_of(ctxw + j * frames, frames)
            return (kbuf if arr == K else vbuf).at[p, pl.ds(start, frames), :]
        start = pl.multiple_of(j * frames, frames)
        return (qbuf if arr == Q else gbuf).at[p, pl.ds(start, frames), :]

    def local_in(arr, p):
        return pltpu.make_async_copy(srcs[arr].at[0, :, lanes(i, p)], rows_of(arr, p, i), loc_sem.at[arr, p])

    def a_copy(arr, p, j):
        return pltpu.make_async_remote_copy(
            src_ref=srcs[arr].at[0, :, lanes(j, p)],
            dst_ref=rows_of(arr, p, i),
            send_sem=a_send.at[arr, p, j],
            recv_sem=a_recv.at[arr, p, i],
            device_id=group_dev(j),
            device_id_type=MESH,
        )

    def a_arrival(arr, p, j):
        return pltpu.make_async_remote_copy(
            src_ref=rows_of(arr, p, j),
            dst_ref=rows_of(arr, p, j),
            send_sem=a_send.at[arr, p, j],
            recv_sem=a_recv.at[arr, p, j],
            device_id=group_dev(j),
            device_id_type=MESH,
        )

    def halo_copy(a, p, direction):
        buf = (kbuf, vbuf)[a]
        src = own if direction else ctxw
        dst = 0 if direction else ctxw + own
        return pltpu.make_async_remote_copy(
            src_ref=buf.at[p, pl.ds(src, ctxw), :],
            dst_ref=buf.at[p, pl.ds(dst, ctxw), :],
            send_sem=h_send.at[a, p, direction],
            recv_sem=h_recv.at[a, p, direction],
            device_id=side_dev(direction),
            device_id_type=MESH,
        )

    def grad_copy(a, p, direction):
        return pltpu.make_async_remote_copy(
            src_ref=halo_out.at[a, p, direction],
            dst_ref=halo_in.at[a, p, direction],
            send_sem=g_send.at[a, p, direction],
            recv_sem=g_recv.at[a, p, direction],
            device_id=side_dev(direction),
            device_id_type=MESH,
        )

    def out_copy(arr, p, j):
        return pltpu.make_async_remote_copy(
            src_ref=ostage.at[arr, p, j],
            dst_ref=outs[arr].at[0, :, lanes(i, p)],
            send_sem=o_send.at[arr, p, j],
            recv_sem=o_recv.at[arr, p, i],
            device_id=group_dev(j),
            device_id_type=MESH,
        )

    def out_arrival(arr, p, j):
        return pltpu.make_async_remote_copy(
            src_ref=ostage.at[arr, p, j],
            dst_ref=outs[arr].at[0, :, lanes(j, p)],
            send_sem=o_send.at[arr, p, j],
            recv_sem=o_recv.at[arr, p, j],
            device_id=group_dev(j),
            device_id_type=MESH,
        )

    def out_local(arr, p):
        return pltpu.make_async_copy(ostage.at[arr, p, i], outs[arr].at[0, :, lanes(i, p)], o_loc.at[arr, p])

    def send_out(arr, p, j):
        @pl.when(j != i)
        def _():
            out_copy(arr, p, j).start()

        @pl.when(j == i)
        def _():
            out_local(arr, p).start()

    def b1_copy(p, s):
        return pltpu.make_async_remote_copy(
            src_ref=b1buf.at[slot, p],
            dst_ref=b1buf.at[slot, p],
            send_sem=b1_send.at[p, s],
            recv_sem=b1_recv.at[p, slot],
            device_id=peer_dev(s),
            device_id_type=MESH,
        )

    def b1_arrival(p, s):
        return pltpu.make_async_remote_copy(
            src_ref=b1buf.at[s, p],
            dst_ref=b1buf.at[s, p],
            send_sem=b1_send.at[p, s],
            recv_sem=b1_recv.at[p, s],
            device_id=peer_dev(s),
            device_id_type=MESH,
        )

    def b2_copy(p, j):
        return pltpu.make_async_remote_copy(
            src_ref=sum_buf.at[p],
            dst_ref=b2buf.at[i, p],
            send_sem=b2_send.at[p, j],
            recv_sem=b2_recv.at[p, i],
            device_id=group_dev(j),
            device_id_type=MESH,
        )

    def b2_arrival(p, j):
        return pltpu.make_async_remote_copy(
            src_ref=sum_buf.at[p],
            dst_ref=b2buf.at[j, p],
            send_sem=b2_send.at[p, j],
            recv_sem=b2_recv.at[p, j],
            device_id=group_dev(j),
            device_id_type=MESH,
        )

    def others(fn):
        for s in range(1, GROUP):
            fn(lax.rem(i + s, GROUP))

    def all_peers(fn):
        def step(t, carry):
            fn(lax.rem(slot + t, n_peer))
            return carry

        lax.fori_loop(1, n_peer, step, 0)

    barrier = pltpu.get_barrier_semaphore()

    def greet(device):
        pl.semaphore_signal(barrier, inc=1, device_id=device, device_id_type=MESH)

    others(lambda j: greet(group_dev(j)))
    all_peers(lambda s: greet(peer_dev(s)))
    for p in range(PAIRS):
        for arr in (K, V, Q, G):
            local_in(arr, p).start()
    pl.semaphore_wait(barrier, GROUP - 1 + n_peer - 1)

    for p in range(PAIRS):
        for arr in (K, V, Q, G):
            others(lambda j: a_copy(arr, p, j).start())

    for p in range(PAIRS):
        for h in range(2):
            row = rev_ref[pl.ds(i * (2 * PAIRS) + 2 * p + h, 1), :]
            table = jnp.broadcast_to(row, (frames, span))
            bias_tab[p, h * frames : (h + 1) * frames, :] = pltpu.roll(
                table, 0, 1, stride=1, stride_axis=0
            )
    bias_acc[...] = jnp.zeros_like(bias_acc)
    gk_acc[...] = jnp.zeros_like(gk_acc)
    gv_acc[...] = jnp.zeros_like(gv_acc)
    edge_zero = jnp.zeros((PAIRS, ctxw, LANES), jnp.bfloat16)

    @pl.when(jnp.logical_not(has_lo))
    def _():
        kbuf[:, :ctxw, :] = edge_zero
        vbuf[:, :ctxw, :] = edge_zero

    @pl.when(jnp.logical_not(has_hi))
    def _():
        kbuf[:, ctxw + own :, :] = edge_zero
        vbuf[:, ctxw + own :, :] = edge_zero

    def forward_halo(p):
        for a, arr in enumerate((K, V)):
            local_in(arr, p).wait()
            others(lambda j: a_arrival(arr, p, j).wait_recv())

            @pl.when(has_lo)
            def _():
                halo_copy(a, p, 0).start()

            @pl.when(has_hi)
            def _():
                halo_copy(a, p, 1).start()

    def wait_inputs(p):
        for arr in (Q, G):
            local_in(arr, p).wait()
            others(lambda j: a_arrival(arr, p, j).wait_recv())
        for a in range(2):
            @pl.when(has_lo)
            def _():
                halo_copy(a, p, 1).wait_recv()

            @pl.when(has_hi)
            def _():
                halo_copy(a, p, 0).wait_recv()

    low = lax.broadcasted_iota(jnp.int32, (frames, LANES), 1) < HEAD

    def stack_heads(x):
        zero = jnp.zeros_like(x)
        return jnp.concatenate([jnp.where(low, x, zero), jnp.where(low, zero, x)], axis=0)

    def merge_heads(x):
        return jnp.where(low, x[:frames], x[frames:])

    column = lax.broadcasted_iota(jnp.int32, (1, span), 1)

    def unit(p, b):
        r0 = pl.multiple_of(b * frames, frames)
        own_rows = pl.ds(r0, frames)
        window = pl.ds(r0, span)
        key_row = column + ((g * GROUP - NB + b) * frames)
        exists = (key_row >= 0) & (key_row < n_groups * own)
        edge = jnp.where(exists, 0.0, EXCLUDED).astype(jnp.float32)
        kw = kbuf[p, window, :]
        vw = vbuf[p, window, :]
        qs = stack_heads(qbuf[p, own_rows, :].astype(jnp.float32) * score_scale).astype(jnp.bfloat16)
        gs = stack_heads(gbuf[p, own_rows, :].astype(jnp.float32)).astype(jnp.bfloat16)
        scores = dot(qs, kw, NT) + bias_tab[p] + edge
        top = jnp.max(scores, axis=1, keepdims=True)
        expd = jnp.exp(scores - top)
        total = jnp.sum(expd, axis=1, keepdims=True)
        probs = expd * (1.0 / total)
        weights = probs.astype(jnp.bfloat16)
        attended = merge_heads(dot(weights, vw)).astype(jnp.bfloat16)
        ostage[0, p, b] = attended
        send_out(0, p, b)
        wide = attended.astype(jnp.float32)
        delta = jnp.sum(
            gs.astype(jnp.float32) * jnp.concatenate([wide, wide], axis=0), axis=1, keepdims=True
        )
        dscore = probs * (dot(gs, vw, NT) - delta)
        dscore_low = dscore.astype(jnp.bfloat16)
        bias_acc[p] += dscore
        grad_q = merge_heads(dot(dscore_low, kw)) * score_scale
        ostage[1, p, b] = grad_q.astype(jnp.bfloat16)
        send_out(1, p, b)
        gk_acc[p, window, :] += dot(dscore_low, qs, TN)
        gv_acc[p, window, :] += dot(weights, gs, TN)

    def send_grads(p):
        for a in range(2):
            @pl.when(has_lo)
            def _():
                halo_out[a, p, 0] = accs[a][p, :ctxw, :].astype(jnp.bfloat16)
                grad_copy(a, p, 0).start()

            @pl.when(has_hi)
            def _():
                halo_out[a, p, 1] = accs[a][p, ctxw + own :, :].astype(jnp.bfloat16)
                grad_copy(a, p, 1).start()

    def send_bias(p):
        sub = lax.broadcasted_iota(jnp.int32, (8, span), 0)
        b1buf[slot, p] = jnp.zeros((16, 128), jnp.float32)
        for h in range(2):
            part = bias_acc[p, h * frames : (h + 1) * frames, :]
            rows = frames
            while rows > 8:
                rows //= 2
                part = part[:rows] + pltpu.roll(part[rows:], span - rows, 1)
            for s in (4, 2, 1):
                part = jnp.where((sub & s) != 0, pltpu.roll(part, span - s, 1), part)
            diag = jnp.sum(part, axis=0, keepdims=True)
            for c in range(span // 128):
                n = h * (span // 128) + c
                b1buf[slot, p, n : n + 1, :] = diag[:, c * 128 : (c + 1) * 128]
        all_peers(lambda s: b1_copy(p, s).start())

    def sum_bias(p):
        all_peers(lambda s: b1_arrival(p, s).wait_recv())
        sum_buf[p] = lax.fori_loop(
            0, n_peer, lambda s, acc: acc + b1buf[s, p], jnp.zeros((16, 128), jnp.float32)
        )
        others(lambda j: b2_copy(p, j).start())
        b2buf[i, p] = sum_buf[p]

    def finish_grads(p):
        for a in range(2):
            acc = accs[a]

            @pl.when(has_lo)
            def _():
                grad_copy(a, p, 1).wait_recv()
                acc[p, ctxw : 2 * ctxw, :] += halo_in[a, p, 1].astype(jnp.float32)

            @pl.when(has_hi)
            def _():
                grad_copy(a, p, 0).wait_recv()
                acc[p, own : own + ctxw, :] += halo_in[a, p, 0].astype(jnp.float32)

            for j in range(GROUP):
                start = ctxw + j * frames
                ostage[2 + a, p, j] = acc[p, start : start + frames, :].astype(jnp.bfloat16)
                send_out(2 + a, p, j)

    forward_halo(0)
    for p in range(PAIRS):
        wait_inputs(p)

        def step(b, carry):
            unit(p, b)

            @pl.when(b == 1)
            def _():
                if p + 1 < PAIRS:
                    forward_halo(p + 1)
                if p > 0:
                    sum_bias(p - 1)
                    finish_grads(p - 1)

            return carry

        lax.fori_loop(0, GROUP, step, 0)
        send_grads(p)
        send_bias(p)
    finish_grads(PAIRS - 1)
    sum_bias(PAIRS - 1)

    for p in range(PAIRS):
        others(lambda j: b2_arrival(p, j).wait_recv())
    bias_out[...] = b2buf[...]
    for p in range(PAIRS):
        for arr in range(4):
            others(lambda j: out_arrival(arr, p, j).wait_recv())
            out_local(arr, p).wait()
            others(lambda j: out_copy(arr, p, j).wait_send())
            others(lambda j: a_copy(arr, p, j).wait_send())
        for a in range(2):
            @pl.when(has_lo)
            def _():
                halo_copy(a, p, 0).wait_send()
                grad_copy(a, p, 0).wait_send()

            @pl.when(has_hi)
            def _():
                halo_copy(a, p, 1).wait_send()
                grad_copy(a, p, 1).wait_send()

        all_peers(lambda s: b1_copy(p, s).wait_send())
        others(lambda j: b2_copy(p, j).wait_send())


def body(queries, keys, values, rel_bias, grad_out):
    rec_dev, frames, width = queries.shape
    n_dp = lax.axis_size("dp")
    n_groups = lax.axis_size("ctx") // GROUP
    n_peer = n_dp * n_groups
    span = (2 * NB + 1) * frames
    ctxw = NB * frames
    own = GROUP * frames
    rows = own + 2 * ctxw
    count = 2 * ctxw + 1
    reversed_bias = jnp.pad(
        rel_bias[:, ::-1], ((0, 0), (0, span - count)), constant_values=EXCLUDED
    )
    block = jax.ShapeDtypeStruct(queries.shape, jnp.bfloat16)
    bf16, f32 = jnp.bfloat16, jnp.float32
    dma = pltpu.SemaphoreType.DMA
    hbm = pl.BlockSpec(memory_space=pl.ANY)
    vmem = pl.BlockSpec(memory_space=pltpu.VMEM)
    macs = 6 * GROUP * frames * span * 2 * PAIRS * HEAD
    att, gq, gk, gv, bias = pl.pallas_call(
        functools.partial(kernel, n_dp, n_groups, frames),
        out_shape=(block, block, block, block, jax.ShapeDtypeStruct((GROUP, PAIRS, 16, 128), f32)),
        in_specs=[hbm, hbm, hbm, hbm, vmem],
        out_specs=(hbm, hbm, hbm, hbm, vmem),
        scratch_shapes=[
            pltpu.VMEM((PAIRS, own, LANES), bf16),
            pltpu.VMEM((PAIRS, own, LANES), bf16),
            pltpu.VMEM((PAIRS, rows, LANES), bf16),
            pltpu.VMEM((PAIRS, rows, LANES), bf16),
            pltpu.VMEM((PAIRS, 2 * frames, span), f32),
            pltpu.VMEM((PAIRS, 2 * frames, span), f32),
            pltpu.VMEM((PAIRS, rows, LANES), f32),
            pltpu.VMEM((PAIRS, rows, LANES), f32),
            pltpu.VMEM((2, PAIRS, 2, ctxw, LANES), bf16),
            pltpu.VMEM((2, PAIRS, 2, ctxw, LANES), bf16),
            pltpu.VMEM((4, PAIRS, GROUP, frames, LANES), bf16),
            pltpu.VMEM((n_peer, PAIRS, 16, 128), f32),
            pltpu.VMEM((GROUP, PAIRS, 16, 128), f32),
            pltpu.VMEM((PAIRS, 16, 128), f32),
            dma((4, PAIRS)),
            dma((4, PAIRS, GROUP)),
            dma((4, PAIRS, GROUP)),
            dma((2, PAIRS, 2)),
            dma((2, PAIRS, 2)),
            dma((2, PAIRS, 2)),
            dma((2, PAIRS, 2)),
            dma((4, PAIRS, GROUP)),
            dma((4, PAIRS, GROUP)),
            dma((4, PAIRS)),
            dma((PAIRS, n_peer)),
            dma((PAIRS, n_peer)),
            dma((PAIRS, GROUP)),
            dma((PAIRS, GROUP)),
        ],
        compiler_params=pltpu.CompilerParams(
            collective_id=0, has_side_effects=True, vmem_limit_bytes=48 * 1024 * 1024
        ),
        cost_estimate=pl.CostEstimate(
            flops=2 * macs, bytes_accessed=8 * frames * width * 2, transcendentals=own * span * 2 * PAIRS
        ),
    )(queries, keys, values, grad_out, reversed_bias)
    tiles = 2 * (span // 128)
    table = bias[:, :, :tiles, :].reshape(HEADS, span)
    grad_bias = table[:, :count][:, ::-1]
    return (att, gq, gk, gv, grad_bias)


def solution(mesh):
    placed = (
        P("dp", "ctx", None),
        P("dp", "ctx", None),
        P("dp", "ctx", None),
        P(),
        P("dp", "ctx", None),
    )
    return jax.shard_map(
        body,
        mesh=mesh,
        in_specs=placed,
        out_specs=(
            P("dp", "ctx", None),
            P("dp", "ctx", None),
            P("dp", "ctx", None),
            P("dp", "ctx", None),
            P(),
        ),
        check_vma=False,
    )
```

```python
import functools
import math

import jax
import jax.numpy as jnp
from jax import lax
from jax.experimental import pallas as pl
from jax.experimental.pallas import tpu as pltpu
from jax.sharding import PartitionSpec as P

HEADS = 16
HEAD = 64
NB = 3
GROUP = 4
PAIRS = HEADS // GROUP // 2
LANES = 2 * HEAD
EXCLUDED = -1e30
VMEM_LIMIT = 60 * 1024 * 1024
MESH = pl.DeviceIdType.MESH
Q, K, V, G = 0, 1, 2, 3
NT = (((1,), (1,)), ((), ()))


ORDER = (0, 3, 1, 2)
DONE = {0: ((0, 0),), 3: ((1, 2),), 1: ((0, 1),), 2: ((1, 0), (1, 1), (0, 2))}


def dot(a, b, dims=(((1,), (0,)), ((), ()))):
    return lax.dot_general(a, b, dims, preferred_element_type=jnp.float32)


def mirror_lanes(x):
    row = lax.broadcasted_iota(jnp.int32, (128, 128), 0)
    col = lax.broadcasted_iota(jnp.int32, (128, 128), 1)
    exchange = (row + col == 127).astype(jnp.float32)
    return jnp.dot(
        x, exchange, precision=lax.Precision.HIGHEST, preferred_element_type=jnp.float32
    )


def kernel(
    n_dp, n_groups, frames,
    q_hbm, k_hbm, v_hbm, g_hbm, rel_ref,
    att_out, gq_out, gk_out, gv_out, bias_out,
    qbuf, gbuf, kbuf, vbuf, rev_buf, bias_tab, bias_acc, gk_acc, gv_acc,
    ds_buf, w_buf, qt_buf, gt_buf, halo_out, halo_in, ostage, b1buf, sum_buf,
    loc_sem, a_send, a_recv, h_send, h_recv, g_send, g_recv,
    o_send, o_recv, o_loc, b1_send, b1_recv, b2_send, b2_recv,
):
    span = (2 * NB + 1) * frames
    ctxw = NB * frames
    own = GROUP * frames
    score_scale = 1.0 / math.sqrt(HEAD)
    dp = lax.axis_index("dp")
    ctx = lax.axis_index("ctx")
    g = lax.div(ctx, GROUP)
    i = lax.rem(ctx, GROUP)
    n_peer = n_dp * n_groups
    slot = dp * n_groups + g
    has_lo = g > 0
    has_hi = g < n_groups - 1
    srcs = (q_hbm, k_hbm, v_hbm, g_hbm)
    outs = (att_out, gq_out, gk_out, gv_out)
    accs = (gk_acc, gv_acc)

    def group_dev(j):
        return {"dp": dp, "ctx": g * GROUP + j}

    def side_dev(direction):
        return {"dp": dp, "ctx": ctx + (GROUP if direction else -GROUP)}

    def peer_dev(s):
        return {"dp": lax.div(s, n_groups), "ctx": lax.rem(s, n_groups) * GROUP + i}

    def lanes(j, p):
        return pl.ds(pl.multiple_of((j * PAIRS + p) * LANES, LANES), LANES)

    def rows_of(arr, p, j):
        if arr in (K, V):
            start = pl.multiple_of(ctxw + j * frames, frames)
            return (kbuf if arr == K else vbuf).at[p, pl.ds(start, frames), :]
        start = pl.multiple_of(j * frames, frames)
        return (qbuf if arr == Q else gbuf).at[p, pl.ds(start, frames), :]

    def local_in(arr, p):
        return pltpu.make_async_copy(srcs[arr].at[0, :, lanes(i, p)], rows_of(arr, p, i), loc_sem.at[arr, p])

    def a_copy(arr, p, j):
        return pltpu.make_async_remote_copy(
            src_ref=srcs[arr].at[0, :, lanes(j, p)],
            dst_ref=rows_of(arr, p, i),
            send_sem=a_send.at[arr, p, j],
            recv_sem=a_recv.at[arr, p, i],
            device_id=group_dev(j),
            device_id_type=MESH,
        )

    def a_arrival(arr, p, j):
        return pltpu.make_async_remote_copy(
            src_ref=rows_of(arr, p, j),
            dst_ref=rows_of(arr, p, j),
            send_sem=a_send.at[arr, p, j],
            recv_sem=a_recv.at[arr, p, j],
            device_id=group_dev(j),
            device_id_type=MESH,
        )

    def halo_copy(a, p, direction, j):
        buf = (kbuf, vbuf)[a]
        src = pl.multiple_of(ctxw + j * frames, frames)
        place = j - 1 if direction else j
        dst = pl.multiple_of(place * frames + (0 if direction else ctxw + own), frames)
        return pltpu.make_async_remote_copy(
            src_ref=buf.at[p, pl.ds(src, frames), :],
            dst_ref=buf.at[p, pl.ds(dst, frames), :],
            send_sem=h_send.at[a, p, direction, place],
            recv_sem=h_recv.at[a, p, direction, place],
            device_id=side_dev(direction),
            device_id_type=MESH,
        )

    def grad_copy(a, p, direction, blk):
        return pltpu.make_async_remote_copy(
            src_ref=halo_out.at[a, p, direction, blk],
            dst_ref=halo_in.at[a, p, direction, blk],
            send_sem=g_send.at[a, p, direction, blk],
            recv_sem=g_recv.at[a, p, direction, blk],
            device_id=side_dev(direction),
            device_id_type=MESH,
        )

    def out_copy(arr, p, j):
        return pltpu.make_async_remote_copy(
            src_ref=ostage.at[arr, p, j],
            dst_ref=outs[arr].at[0, :, lanes(i, p)],
            send_sem=o_send.at[arr, p, j],
            recv_sem=o_recv.at[arr, p, i],
            device_id=group_dev(j),
            device_id_type=MESH,
        )

    def out_arrival(arr, p, j):
        return pltpu.make_async_remote_copy(
            src_ref=ostage.at[arr, p, j],
            dst_ref=outs[arr].at[0, :, lanes(j, p)],
            send_sem=o_send.at[arr, p, j],
            recv_sem=o_recv.at[arr, p, j],
            device_id=group_dev(j),
            device_id_type=MESH,
        )

    def out_local(arr, p):
        return pltpu.make_async_copy(ostage.at[arr, p, i], outs[arr].at[0, :, lanes(i, p)], o_loc.at[arr, p])

    def send_out(arr, p, j):
        @pl.when(j != i)
        def _():
            out_copy(arr, p, j).start()

        @pl.when(j == i)
        def _():
            out_local(arr, p).start()

    def b1_copy(p, s):
        return pltpu.make_async_remote_copy(
            src_ref=b1buf.at[slot, p],
            dst_ref=b1buf.at[slot, p],
            send_sem=b1_send.at[p, s],
            recv_sem=b1_recv.at[p, slot],
            device_id=peer_dev(s),
            device_id_type=MESH,
        )

    def b1_arrival(p, s):
        return pltpu.make_async_remote_copy(
            src_ref=b1buf.at[s, p],
            dst_ref=b1buf.at[s, p],
            send_sem=b1_send.at[p, s],
            recv_sem=b1_recv.at[p, s],
            device_id=peer_dev(s),
            device_id_type=MESH,
        )

    def b2_copy(p, j):
        return pltpu.make_async_remote_copy(
            src_ref=sum_buf.at[p],
            dst_ref=bias_out.at[i, p],
            send_sem=b2_send.at[p, j],
            recv_sem=b2_recv.at[p, i],
            device_id=group_dev(j),
            device_id_type=MESH,
        )

    def b2_arrival(p, j):
        return pltpu.make_async_remote_copy(
            src_ref=sum_buf.at[p],
            dst_ref=bias_out.at[j, p],
            send_sem=b2_send.at[p, j],
            recv_sem=b2_recv.at[p, j],
            device_id=group_dev(j),
            device_id_type=MESH,
        )

    def others(fn):
        core = lax.rem(i, 2)
        far = 2 - 2 * lax.div(i, 2)
        fn(i + 1 - 2 * core)
        fn(far + core)
        fn(far + 1 - core)

    def all_peers(fn):
        def step(t, carry):
            fn(lax.rem(slot + t, n_peer))
            return carry

        lax.fori_loop(1, n_peer, step, 0)

    barrier = pltpu.get_barrier_semaphore()

    def greet(device):
        pl.semaphore_signal(barrier, inc=1, device_id=device, device_id_type=MESH)

    others(lambda j: greet(group_dev(j)))
    all_peers(lambda s: greet(peer_dev(s)))
    for p in range(PAIRS):
        for arr in (K, V, Q, G):
            local_in(arr, p).start()
    pl.semaphore_wait(barrier, GROUP - 1 + n_peer - 1)

    for p in range(PAIRS):
        for arr in (K, V, Q, G):
            others(lambda j: a_copy(arr, p, j).start())

    chunks = 2 * ctxw // 128
    for c in range(chunks):
        rev_buf[:, (chunks - 1 - c) * 128 : (chunks - c) * 128] = mirror_lanes(
            rel_ref[:, c * 128 : (c + 1) * 128]
        )
    last_lane = lax.broadcasted_iota(jnp.int32, (HEADS, 128), 1) == 127
    rev_buf[:, 2 * ctxw :] = jnp.where(
        last_lane, rel_ref[:, 2 * ctxw : 2 * ctxw + 1], jnp.float32(EXCLUDED)
    )
    for p in range(PAIRS):
        for h in range(2):
            row = rev_buf[pl.ds(i * (2 * PAIRS) + 2 * p + h, 1), :]
            table = jnp.broadcast_to(row, (frames, span))
            bias_tab[p, h * frames : (h + 1) * frames, :] = pltpu.roll(
                table, 1, 1, stride=1, stride_axis=0
            )
    bias_acc[...] = jnp.zeros_like(bias_acc)
    gk_acc[...] = jnp.zeros_like(gk_acc)
    gv_acc[...] = jnp.zeros_like(gv_acc)
    edge_zero = jnp.zeros((PAIRS, ctxw, LANES), jnp.bfloat16)
    edge_grad = jnp.zeros((2, PAIRS, NB, LANES, frames), jnp.bfloat16)

    @pl.when(jnp.logical_not(has_lo))
    def _():
        kbuf[:, :ctxw, :] = edge_zero
        vbuf[:, :ctxw, :] = edge_zero
        halo_in[:, :, 1] = edge_grad

    @pl.when(jnp.logical_not(has_hi))
    def _():
        kbuf[:, ctxw + own :, :] = edge_zero
        vbuf[:, ctxw + own :, :] = edge_zero
        halo_in[:, :, 0] = edge_grad

    def forward_halo(p):
        def forward(a, j):
            @pl.when(has_lo & (j < NB))
            def _():
                halo_copy(a, p, 0, j).start()

            @pl.when(has_hi & (j > 0))
            def _():
                halo_copy(a, p, 1, j).start()

        for a, arr in enumerate((K, V)):
            local_in(arr, p).wait()
            forward(a, i)

        def passed_on(j):
            for a, arr in enumerate((K, V)):
                a_arrival(arr, p, j).wait_recv()
                forward(a, j)

        others(passed_on)

    def wait_inputs(p):
        for arr in (Q, G):
            local_in(arr, p).wait()
            others(lambda j: a_arrival(arr, p, j).wait_recv())
        for a in range(2):
            @pl.when(has_lo)
            def _():
                for j in range(1, GROUP):
                    halo_copy(a, p, 1, j).wait_recv()

            @pl.when(has_hi)
            def _():
                for j in range(NB):
                    halo_copy(a, p, 0, j).wait_recv()

    low = lax.broadcasted_iota(jnp.int32, (frames, LANES), 1) < HEAD

    def stack_heads(x):
        zero = jnp.zeros_like(x)
        return jnp.concatenate([jnp.where(low, x, zero), jnp.where(low, zero, x)], axis=0)

    def merge_heads(x):
        return jnp.where(low, x[:frames], x[frames:])

    column = lax.broadcasted_iota(jnp.int32, (1, span), 1)

    top_half = lax.broadcasted_iota(jnp.int32, (LANES, frames), 0) < HEAD

    def stack_turned(x):
        turned = x.T
        zero = jnp.zeros_like(turned)
        return jnp.concatenate(
            [jnp.where(top_half, turned, zero), jnp.where(top_half, zero, turned)], axis=1
        ).astype(jnp.bfloat16)

    def softmax_part(n, p, b):
        own_rows = slice(b * frames, (b + 1) * frames)
        window = slice(b * frames, b * frames + span)
        key_row = column + ((g * GROUP - NB + b) * frames)
        exists = (key_row >= 0) & (key_row < n_groups * own)
        edge = jnp.where(exists, 0.0, EXCLUDED).astype(jnp.float32)
        kw = kbuf[p, window, :]
        vw = vbuf[p, window, :]
        q32 = qbuf[p, own_rows, :].astype(jnp.float32) * score_scale
        g32 = gbuf[p, own_rows, :].astype(jnp.float32)
        qs = stack_heads(q32).astype(jnp.bfloat16)
        gs32 = stack_heads(g32)
        gs = gs32.astype(jnp.bfloat16)
        qt_buf[n % 2] = stack_turned(q32)
        gt_buf[n % 2] = stack_turned(g32)
        scores = dot(qs, kw, NT) + bias_tab[p] + edge
        top = jnp.max(scores, axis=1, keepdims=True)
        expd = jnp.exp(scores - top)
        total = jnp.sum(expd, axis=1, keepdims=True)
        probs = expd * (1.0 / total)
        weights = probs.astype(jnp.bfloat16)
        w_buf[n % 2] = weights
        attended = merge_heads(dot(weights, vw)).astype(jnp.bfloat16)
        ostage[0, p, b] = attended
        wide = attended.astype(jnp.float32)
        delta = jnp.sum(gs32 * jnp.concatenate([wide, wide], axis=0), axis=1, keepdims=True)
        dscore = probs * (dot(gs, vw, NT) - delta)
        ds_buf[n % 2] = dscore.astype(jnp.bfloat16)
        bias_acc[p] += dscore

    def grad_part(n, p, b):
        window = slice(b * frames, b * frames + span)
        dscore_low = ds_buf[n % 2]
        grad_q = merge_heads(dot(dscore_low, kbuf[p, window, :])) * score_scale
        ostage[1, p, b] = grad_q.astype(jnp.bfloat16)
        gk_acc[p, :, window] += dot(qt_buf[n % 2], dscore_low)
        gv_acc[p, :, window] += dot(gt_buf[n % 2], w_buf[n % 2])

    def send_grads(p, b):
        send_out(1, p, b)
        for direction, blk in DONE[b]:
            start = blk * frames + (ctxw + own if direction else 0)

            @pl.when(has_hi if direction else has_lo)
            def _():
                for a in range(2):
                    halo_out[a, p, direction, blk] = accs[a][p, :, start : start + frames].astype(
                        jnp.bfloat16
                    )
                    grad_copy(a, p, direction, blk).start()

    def send_bias(p):
        sub = lax.broadcasted_iota(jnp.int32, (8, span), 0)
        b1buf[slot, p] = jnp.zeros((16, 128), jnp.float32)
        for h in range(2):
            part = bias_acc[p, h * frames : (h + 1) * frames, :]
            rows = frames
            while rows > 8:
                rows //= 2
                part = part[:rows] + pltpu.roll(part[rows:], span - rows, 1)
            for s in (4, 2, 1):
                part = jnp.where((sub & s) != 0, pltpu.roll(part, span - s, 1), part)
            diag = pltpu.roll(jnp.sum(part, axis=0, keepdims=True), span - 1, 1)
            for c in range(span // 128):
                n = h * (span // 128) + c
                b1buf[slot, p, n : n + 1, :] = diag[:, c * 128 : (c + 1) * 128]
        all_peers(lambda s: b1_copy(p, s).start())

    def sum_bias(p):
        all_peers(lambda s: b1_arrival(p, s).wait_recv())
        sum_buf[p] = lax.fori_loop(
            0, n_peer, lambda s, acc: acc + b1buf[s, p], jnp.zeros((16, 128), jnp.float32)
        )
        others(lambda j: b2_copy(p, j).start())
        bias_out[i, p] = sum_buf[p]

    def finish_grads(p):
        for j in (2, 0, 1, 3):
            for a in range(2):
                if j < NB:
                    @pl.when(has_lo)
                    def _():
                        grad_copy(a, p, 1, j).wait_recv()
                if j > 0:
                    @pl.when(has_hi)
                    def _():
                        grad_copy(a, p, 0, j - 1).wait_recv()
                start = ctxw + j * frames
                full = accs[a][p, :, start : start + frames]
                if j < NB:
                    full = full + halo_in[a, p, 1, j].astype(jnp.float32)
                if j > 0:
                    full = full + halo_in[a, p, 0, j - 1].astype(jnp.float32)
                ostage[2 + a, p, j] = full.T.astype(jnp.bfloat16)
                send_out(2 + a, p, j)

    units = [(p, b) for p in range(PAIRS) for b in ORDER]
    forward_halo(0)
    for n, (p, b) in enumerate(units):
        if b == ORDER[0]:
            wait_inputs(p)
        softmax_part(n, p, b)
        if n > 0:
            grad_part(n - 1, *units[n - 1])
        send_out(0, p, b)
        if n > 0:
            send_grads(*units[n - 1])
        if b == ORDER[0]:
            if p + 1 < PAIRS:
                forward_halo(p + 1)
            if p > 0:
                send_bias(p - 1)
        if b == ORDER[2] and p > 0:
            sum_bias(p - 1)
            finish_grads(p - 1)
    send_bias(PAIRS - 1)
    grad_part(len(units) - 1, *units[-1])
    send_grads(*units[-1])
    sum_bias(PAIRS - 1)
    finish_grads(PAIRS - 1)

    for p in range(PAIRS):
        others(lambda j: b2_arrival(p, j).wait_recv())
    for p in range(PAIRS):
        for arr in range(4):
            others(lambda j: out_arrival(arr, p, j).wait_recv())
            out_local(arr, p).wait()
            others(lambda j: out_copy(arr, p, j).wait_send())
            others(lambda j: a_copy(arr, p, j).wait_send())
        for a in range(2):
            @pl.when(has_lo)
            def _():
                for j in range(NB):
                    halo_copy(a, p, 0, j).wait_send()
                    grad_copy(a, p, 0, j).wait_send()

            @pl.when(has_hi)
            def _():
                for j in range(NB):
                    halo_copy(a, p, 1, j + 1).wait_send()
                    grad_copy(a, p, 1, j).wait_send()

        all_peers(lambda s: b1_copy(p, s).wait_send())
        others(lambda j: b2_copy(p, j).wait_send())


def finish(att, gq, gk, gv, bias, att_out, gq_out, gk_out, gv_out, bias_out, sems):
    copies = [
        pltpu.make_async_copy(src, dst, sems.at[n])
        for n, (src, dst) in enumerate(
            ((att, att_out), (gq, gq_out), (gk, gk_out), (gv, gv_out))
        )
    ]
    for copy in copies:
        copy.start()
    chunks = bias_out.shape[1] // 128
    mirrored = mirror_lanes(bias[...].reshape(GROUP * PAIRS * 16, 128))
    for head in range(HEADS):
        base = (head // 2) * 16 + (head % 2) * (chunks + 1)
        for c in range(chunks):
            place = (chunks - 1 - c) * 128
            bias_out[head : head + 1, place : place + 128] = mirrored[base + c : base + c + 1, :]
        bias_out[head : head + 1, chunks * 128 :] = mirrored[base + chunks : base + chunks + 1, :1]
    for copy in copies:
        copy.wait()


def body(queries, keys, values, rel_bias, grad_out):
    rec_dev, frames, width = queries.shape
    n_dp = lax.axis_size("dp")
    n_groups = lax.axis_size("ctx") // GROUP
    n_peer = n_dp * n_groups
    span = (2 * NB + 1) * frames
    ctxw = NB * frames
    own = GROUP * frames
    rows = own + 2 * ctxw
    block = jax.ShapeDtypeStruct(queries.shape, jnp.bfloat16)
    bf16, f32 = jnp.bfloat16, jnp.float32
    dma = pltpu.SemaphoreType.DMA
    anywhere = pl.BlockSpec(memory_space=pl.ANY)
    hbm = pl.BlockSpec(memory_space=pltpu.HBM)
    vmem = pl.BlockSpec(memory_space=pltpu.VMEM)
    macs = 6 * GROUP * frames * span * 2 * PAIRS * HEAD
    parts = pl.pallas_call(
        functools.partial(kernel, n_dp, n_groups, frames),
        out_shape=(block, block, block, block, jax.ShapeDtypeStruct((GROUP, PAIRS, 16, 128), f32)),
        in_specs=[hbm, hbm, hbm, hbm, vmem],
        out_specs=(anywhere, anywhere, anywhere, anywhere, vmem),
        scratch_shapes=[
            pltpu.VMEM((PAIRS, own, LANES), bf16),
            pltpu.VMEM((PAIRS, own, LANES), bf16),
            pltpu.VMEM((PAIRS, rows, LANES), bf16),
            pltpu.VMEM((PAIRS, rows, LANES), bf16),
            pltpu.VMEM((HEADS, span), f32),
            pltpu.VMEM((PAIRS, 2 * frames, span), f32),
            pltpu.VMEM((PAIRS, 2 * frames, span), f32),
            pltpu.VMEM((PAIRS, LANES, rows), f32),
            pltpu.VMEM((PAIRS, LANES, rows), f32),
            pltpu.VMEM((2, 2 * frames, span), bf16),
            pltpu.VMEM((2, 2 * frames, span), bf16),
            pltpu.VMEM((2, LANES, 2 * frames), bf16),
            pltpu.VMEM((2, LANES, 2 * frames), bf16),
            pltpu.VMEM((2, PAIRS, 2, NB, LANES, frames), bf16),
            pltpu.VMEM((2, PAIRS, 2, NB, LANES, frames), bf16),
            pltpu.VMEM((4, PAIRS, GROUP, frames, LANES), bf16),
            pltpu.VMEM((n_peer, PAIRS, 16, 128), f32),
            pltpu.VMEM((PAIRS, 16, 128), f32),
            dma((4, PAIRS)),
            dma((4, PAIRS, GROUP)),
            dma((4, PAIRS, GROUP)),
            dma((2, PAIRS, 2, NB)),
            dma((2, PAIRS, 2, NB)),
            dma((2, PAIRS, 2, NB)),
            dma((2, PAIRS, 2, NB)),
            dma((4, PAIRS, GROUP)),
            dma((4, PAIRS, GROUP)),
            dma((4, PAIRS)),
            dma((PAIRS, n_peer)),
            dma((PAIRS, n_peer)),
            dma((PAIRS, GROUP)),
            dma((PAIRS, GROUP)),
        ],
        compiler_params=pltpu.CompilerParams(
            collective_id=0, has_side_effects=True, vmem_limit_bytes=VMEM_LIMIT
        ),
        cost_estimate=pl.CostEstimate(
            flops=2 * macs, bytes_accessed=8 * frames * width * 2, transcendentals=own * span * 2 * PAIRS
        ),
    )(queries, keys, values, grad_out, rel_bias)
    return pl.pallas_call(
        finish,
        out_shape=(block, block, block, block, jax.ShapeDtypeStruct(rel_bias.shape, f32)),
        in_specs=[anywhere, anywhere, anywhere, anywhere, vmem],
        out_specs=(hbm, hbm, hbm, hbm, vmem),
        scratch_shapes=[dma((4,))],
        compiler_params=pltpu.CompilerParams(vmem_limit_bytes=VMEM_LIMIT),
        cost_estimate=pl.CostEstimate(
            flops=0, bytes_accessed=8 * frames * width * 2, transcendentals=0
        ),
    )(*parts)


def solution(mesh):
    placed = (
        P("dp", "ctx", None),
        P("dp", "ctx", None),
        P("dp", "ctx", None),
        P(),
        P("dp", "ctx", None),
    )
    return jax.shard_map(
        body,
        mesh=mesh,
        in_specs=placed,
        out_specs=(
            P("dp", "ctx", None),
            P("dp", "ctx", None),
            P("dp", "ctx", None),
            P("dp", "ctx", None),
            P(),
        ),
        check_vma=False,
    )
```

```python
import functools
import math

import jax
import jax.numpy as jnp
from jax import lax
from jax.experimental import pallas as pl
from jax.experimental.pallas import tpu as pltpu
from jax.sharding import PartitionSpec as P

HEADS = 16
HEAD = 64
NB = 3
GROUP = 4
PAIRS = HEADS // GROUP // 2
LANES = 2 * HEAD
EXCLUDED = -1e30
VMEM_LIMIT = 60 * 1024 * 1024
MESH = pl.DeviceIdType.MESH
Q, K, V, G = 0, 1, 2, 3
NT = (((1,), (1,)), ((), ()))


ORDER = (0, 3, 1, 2)
DONE = {0: ((0, 0),), 3: ((1, 2),), 1: ((0, 1),), 2: ((1, 0), (1, 1), (0, 2))}


def dot(a, b, dims=(((1,), (0,)), ((), ()))):
    return lax.dot_general(a, b, dims, preferred_element_type=jnp.float32)


def mirror_lanes(x):
    row = lax.broadcasted_iota(jnp.int32, (128, 128), 0)
    col = lax.broadcasted_iota(jnp.int32, (128, 128), 1)
    exchange = (row + col == 127).astype(jnp.float32)
    return jnp.dot(
        x, exchange, precision=lax.Precision.HIGHEST, preferred_element_type=jnp.float32
    )


def kernel(
    n_dp, n_groups, frames,
    q_hbm, k_hbm, v_hbm, g_hbm, rel_ref,
    parts_out, bias_out,
    qgbuf, kvbuf, rev_buf, bias_tab, bias_acc, gk_acc, gv_acc,
    ds_buf, w_buf, qt_buf, gt_buf, halo_out, halo_in, ostage, b1buf, sum_buf,
    loc_sem, a_send, kv_recv, qg_recv, h_send, h_recv, g_send, g_recv,
    o_send, o_recv, o_loc, b1_send, b1_recv, b2_send, b2_recv,
):
    span = (2 * NB + 1) * frames
    ctxw = NB * frames
    own = GROUP * frames
    score_scale = 1.0 / math.sqrt(HEAD)
    dp = lax.axis_index("dp")
    ctx = lax.axis_index("ctx")
    g = lax.div(ctx, GROUP)
    i = lax.rem(ctx, GROUP)
    n_peer = n_dp * n_groups
    slot = dp * n_groups + g
    has_lo = g > 0
    has_hi = g < n_groups - 1
    srcs = (q_hbm, k_hbm, v_hbm, g_hbm)
    accs = (gk_acc, gv_acc)

    def group_dev(j):
        return {"dp": dp, "ctx": g * GROUP + j}

    def side_dev(direction):
        return {"dp": dp, "ctx": ctx + (GROUP if direction else -GROUP)}

    def peer_dev(s):
        return {"dp": lax.div(s, n_groups), "ctx": lax.rem(s, n_groups) * GROUP + i}

    def lanes(j, p):
        return pl.ds(pl.multiple_of((j * PAIRS + p) * LANES, LANES), LANES)

    def rows_of(arr, p, j):
        if arr in (K, V):
            start = pl.multiple_of(ctxw + j * frames, frames)
            return kvbuf.at[p, arr - K, pl.ds(start, frames), :]
        start = pl.multiple_of(j * frames, frames)
        return qgbuf.at[p, 0 if arr == Q else 1, pl.ds(start, frames), :]

    def local_in(arr, p):
        return pltpu.make_async_copy(srcs[arr].at[0, :, lanes(i, p)], rows_of(arr, p, i), loc_sem.at[arr, p])

    def remote(src, dst, send_sem, recv_sem, device):
        return pltpu.make_async_remote_copy(
            src_ref=src, dst_ref=dst, send_sem=send_sem, recv_sem=recv_sem,
            device_id=device, device_id_type=MESH,
        )

    def a_copy(arr, p, j):
        recv = kv_recv.at[p, i] if arr in (K, V) else qg_recv.at[p]
        return remote(
            srcs[arr].at[0, :, lanes(j, p)], rows_of(arr, p, i), a_send.at[0], recv, group_dev(j)
        )

    def kv_arrival(p, j):
        block = kvbuf.at[p, :, pl.ds(pl.multiple_of(ctxw + j * frames, frames), frames), :]
        return remote(block, block, a_send.at[0], kv_recv.at[p, j], group_dev(j))

    def qg_arrival(p):
        blocks = qgbuf.at[p, :, pl.ds(0, own - frames), :]
        return remote(blocks, blocks, a_send.at[0], qg_recv.at[p], group_dev(i))

    def halo_copy(p, direction, j):
        src = pl.multiple_of(ctxw + j * frames, frames)
        place = j - 1 if direction else j
        dst = pl.multiple_of(place * frames + (0 if direction else ctxw + own), frames)
        return remote(
            kvbuf.at[p, :, pl.ds(src, frames), :],
            kvbuf.at[p, :, pl.ds(dst, frames), :],
            h_send.at[direction], h_recv.at[p, direction], side_dev(direction),
        )

    def halo_arrival(p, direction):
        blocks = kvbuf.at[p, :, pl.ds(0 if direction else ctxw + own, ctxw), :]
        return remote(
            blocks, blocks, h_send.at[direction], h_recv.at[p, direction], side_dev(direction)
        )

    def grad_copy(p, direction, blk):
        return remote(
            halo_out.at[p, direction, blk], halo_in.at[p, direction, blk],
            g_send.at[direction], g_recv.at[p, direction, blk], side_dev(direction),
        )

    def out_parts(half, p, j):
        return ostage.at[p, j, pl.ds(2 * half, 2)]

    def out_copy(half, p, j):
        return remote(
            out_parts(half, p, j), parts_out.at[pl.ds(2 * half, 2), :, lanes(i, p)],
            o_send.at[0], o_recv.at[0], group_dev(j),
        )

    def send_out(half, p, j):
        @pl.when(j != i)
        def _():
            out_copy(half, p, j).start()

        @pl.when(j == i)
        def _():
            pltpu.make_async_copy(
                out_parts(half, p, j), parts_out.at[pl.ds(2 * half, 2), :, lanes(i, p)], o_loc.at[0]
            ).start()

    def b1_copy(p, s):
        return remote(
            b1buf.at[p, slot], b1buf.at[p, slot], b1_send.at[0], b1_recv.at[p], peer_dev(s)
        )

    def b2_copy(p, j):
        return remote(sum_buf.at[p], bias_out.at[p, i], b2_send.at[0], b2_recv.at[p], group_dev(j))

    def others(fn):
        core = lax.rem(i, 2)
        far = 2 - 2 * lax.div(i, 2)
        fn(i + 1 - 2 * core)
        fn(far + core)
        fn(far + 1 - core)

    def all_peers(fn):
        def step(t, carry):
            fn(lax.rem(slot + t, n_peer))
            return carry

        lax.fori_loop(1, n_peer, step, 0)

    barrier = pltpu.get_barrier_semaphore()

    def greet(device):
        pl.semaphore_signal(barrier, inc=1, device_id=device, device_id_type=MESH)

    others(lambda j: greet(group_dev(j)))
    all_peers(lambda s: greet(peer_dev(s)))
    for p in range(PAIRS):
        for arr in (K, V, Q, G):
            local_in(arr, p).start()

    bias_acc[...] = jnp.zeros_like(bias_acc)
    gk_acc[...] = jnp.zeros_like(gk_acc)
    gv_acc[...] = jnp.zeros_like(gv_acc)
    edge_zero = jnp.zeros((PAIRS, 2, ctxw, LANES), jnp.bfloat16)
    edge_grad = jnp.zeros((PAIRS, NB, 2, LANES, frames), jnp.bfloat16)

    @pl.when(jnp.logical_not(has_lo))
    def _():
        kvbuf[:, :, :ctxw, :] = edge_zero
        halo_in[:, 1] = edge_grad

    @pl.when(jnp.logical_not(has_hi))
    def _():
        kvbuf[:, :, ctxw + own :, :] = edge_zero
        halo_in[:, 0] = edge_grad

    pl.semaphore_wait(barrier, GROUP - 1 + n_peer - 1)

    def send_inputs(p):
        for arr in (K, V, Q, G):
            others(lambda j: a_copy(arr, p, j).start())

    send_inputs(0)

    chunks = 2 * ctxw // 128
    for c in range(chunks):
        rev_buf[:, (chunks - 1 - c) * 128 : (chunks - c) * 128] = mirror_lanes(
            rel_ref[:, c * 128 : (c + 1) * 128]
        )
    last_lane = lax.broadcasted_iota(jnp.int32, (HEADS, 128), 1) == 127
    rev_buf[:, 2 * ctxw :] = jnp.where(
        last_lane, rel_ref[:, 2 * ctxw : 2 * ctxw + 1], jnp.float32(EXCLUDED)
    )
    for p in range(PAIRS):
        for h in range(2):
            row = rev_buf[pl.ds(i * (2 * PAIRS) + 2 * p + h, 1), :]
            table = jnp.broadcast_to(row, (frames, span))
            bias_tab[p, h * frames : (h + 1) * frames, :] = pltpu.roll(
                table, 1, 1, stride=1, stride_axis=0
            )
    def forward_halo(p):
        def forward(j):
            @pl.when(has_lo & (j < NB))
            def _():
                halo_copy(p, 0, j).start()

            @pl.when(has_hi & (j > 0))
            def _():
                halo_copy(p, 1, j).start()

        local_in(K, p).wait()
        local_in(V, p).wait()
        forward(i)

        def passed_on(j):
            kv_arrival(p, j).wait_recv()
            forward(j)

        others(passed_on)

    def wait_inputs(p):
        local_in(Q, p).wait()
        local_in(G, p).wait()
        qg_arrival(p).wait_recv()

        @pl.when(has_lo)
        def _():
            halo_arrival(p, 1).wait_recv()

        @pl.when(has_hi)
        def _():
            halo_arrival(p, 0).wait_recv()

    low = lax.broadcasted_iota(jnp.int32, (frames, LANES), 1) < HEAD

    def stack_heads(x):
        zero = jnp.zeros_like(x)
        return jnp.concatenate([jnp.where(low, x, zero), jnp.where(low, zero, x)], axis=0)

    def merge_heads(x):
        return jnp.where(low, x[:frames], x[frames:])

    column = lax.broadcasted_iota(jnp.int32, (1, span), 1)

    top_half = lax.broadcasted_iota(jnp.int32, (LANES, frames), 0) < HEAD

    def stack_turned(x):
        turned = x.T
        zero = jnp.zeros_like(turned)
        return jnp.concatenate(
            [jnp.where(top_half, turned, zero), jnp.where(top_half, zero, turned)], axis=1
        ).astype(jnp.bfloat16)

    def softmax_part(n, p, b):
        own_rows = slice(b * frames, (b + 1) * frames)
        window = slice(b * frames, b * frames + span)
        key_row = column + ((g * GROUP - NB + b) * frames)
        exists = (key_row >= 0) & (key_row < n_groups * own)
        edge = jnp.where(exists, 0.0, EXCLUDED).astype(jnp.float32)
        kw = kvbuf[p, 0, window, :]
        vw = kvbuf[p, 1, window, :]
        q32 = qgbuf[p, 0, own_rows, :].astype(jnp.float32) * score_scale
        g32 = qgbuf[p, 1, own_rows, :].astype(jnp.float32)
        qs = stack_heads(q32).astype(jnp.bfloat16)
        gs32 = stack_heads(g32)
        gs = gs32.astype(jnp.bfloat16)
        qt_buf[n % 2] = stack_turned(q32)
        gt_buf[n % 2] = stack_turned(g32)
        scores = dot(qs, kw, NT) + bias_tab[p] + edge
        top = jnp.max(scores, axis=1, keepdims=True)
        expd = jnp.exp(scores - top)
        total = jnp.sum(expd, axis=1, keepdims=True)
        probs = expd * (1.0 / total)
        weights = probs.astype(jnp.bfloat16)
        w_buf[n % 2] = weights
        attended = merge_heads(dot(weights, vw)).astype(jnp.bfloat16)
        ostage[p, b, 0] = attended
        wide = attended.astype(jnp.float32)
        delta = jnp.sum(gs32 * jnp.concatenate([wide, wide], axis=0), axis=1, keepdims=True)
        dscore = probs * (dot(gs, vw, NT) - delta)
        ds_buf[n % 2] = dscore.astype(jnp.bfloat16)
        bias_acc[p] += dscore

    def grad_part(n, p, b):
        window = slice(b * frames, b * frames + span)
        dscore_low = ds_buf[n % 2]
        grad_q = merge_heads(dot(dscore_low, kvbuf[p, 0, window, :])) * score_scale
        ostage[p, b, 1] = grad_q.astype(jnp.bfloat16)
        gk_acc[p, :, window] += dot(qt_buf[n % 2], dscore_low)
        gv_acc[p, :, window] += dot(gt_buf[n % 2], w_buf[n % 2])

    def send_grads(p, b):
        send_out(0, p, b)
        for direction, blk in DONE[b]:
            start = blk * frames + (ctxw + own if direction else 0)

            @pl.when(has_hi if direction else has_lo)
            def _():
                for a in range(2):
                    halo_out[p, direction, blk, a] = accs[a][p, :, start : start + frames].astype(
                        jnp.bfloat16
                    )
                grad_copy(p, direction, blk).start()

    def send_bias(p):
        sub = lax.broadcasted_iota(jnp.int32, (8, span), 0)
        b1buf[p, slot] = jnp.zeros((16, 128), jnp.float32)
        for h in range(2):
            part = bias_acc[p, h * frames : (h + 1) * frames, :]
            rows = frames
            while rows > 8:
                rows //= 2
                part = part[:rows] + pltpu.roll(part[rows:], span - rows, 1)
            for s in (4, 2, 1):
                part = jnp.where((sub & s) != 0, pltpu.roll(part, span - s, 1), part)
            diag = pltpu.roll(jnp.sum(part, axis=0, keepdims=True), span - 1, 1)
            for c in range(span // 128):
                n = h * (span // 128) + c
                b1buf[p, slot, n : n + 1, :] = diag[:, c * 128 : (c + 1) * 128]
        all_peers(lambda s: b1_copy(p, s).start())

    def sum_bias(p):
        others_part = b1buf.at[p, pl.ds(0, n_peer - 1)]
        remote(
            others_part, others_part, b1_send.at[0], b1_recv.at[p], group_dev(i)
        ).wait_recv()
        sum_buf[p] = lax.fori_loop(
            0, n_peer, lambda s, acc: acc + b1buf[p, s], jnp.zeros((16, 128), jnp.float32)
        )
        others(lambda j: b2_copy(p, j).start())
        bias_out[p, i] = sum_buf[p]

    def finish_grads(p):
        for j in (2, 0, 1, 3):
            if j < NB:
                @pl.when(has_lo)
                def _():
                    grad_copy(p, 1, j).wait_recv()
            if j > 0:
                @pl.when(has_hi)
                def _():
                    grad_copy(p, 0, j - 1).wait_recv()
            start = ctxw + j * frames
            for a in range(2):
                full = accs[a][p, :, start : start + frames]
                if j < NB:
                    full = full + halo_in[p, 1, j, a].astype(jnp.float32)
                if j > 0:
                    full = full + halo_in[p, 0, j - 1, a].astype(jnp.float32)
                ostage[p, j, 2 + a] = full.T.astype(jnp.bfloat16)
            send_out(1, p, j)

    units = [(p, b) for p in range(PAIRS) for b in ORDER]
    forward_halo(0)
    for p in range(1, PAIRS):
        send_inputs(p)
    for n, (p, b) in enumerate(units):
        if b == ORDER[0]:
            wait_inputs(p)
        softmax_part(n, p, b)
        if n > 0:
            grad_part(n - 1, *units[n - 1])
            send_grads(*units[n - 1])
        if b == ORDER[0]:
            if p + 1 < PAIRS:
                forward_halo(p + 1)
            if p > 0:
                send_bias(p - 1)
        if b == ORDER[2] and p > 0:
            sum_bias(p - 1)
            finish_grads(p - 1)
    send_bias(PAIRS - 1)
    grad_part(len(units) - 1, *units[-1])
    send_grads(*units[-1])
    sum_bias(PAIRS - 1)
    finish_grads(PAIRS - 1)

    def drain_send(ref, sem):
        remote(ref, ref, sem, sem, group_dev(i)).wait_send()

    def drain_recv(ref, sem):
        remote(ref, ref, sem, sem, group_dev(i)).wait_recv()

    for p in range(PAIRS):
        drain_recv(bias_out.at[p, pl.ds(0, GROUP - 1)], b2_recv.at[p])
    mine = PAIRS * LANES
    drain_recv(parts_out.at[:, :, pl.ds(0, (GROUP - 1) * mine)], o_recv.at[0])
    own_part = parts_out.at[:, :, pl.ds(0, mine)]
    pltpu.make_async_copy(own_part, own_part, o_loc.at[0]).wait()
    drain_send(parts_out.at[:, :, pl.ds(0, (GROUP - 1) * mine)], o_send.at[0])
    drain_send(parts_out.at[:, :, pl.ds(0, (GROUP - 1) * mine)], a_send.at[0])
    for direction, exists in ((0, has_lo), (1, has_hi)):
        @pl.when(exists)
        def _():
            drain_send(kvbuf.at[:, :, pl.ds(0, ctxw), :], h_send.at[direction])
            drain_send(halo_out.at[:, direction], g_send.at[direction])

    drain_send(b1buf.at[:, pl.ds(0, n_peer - 1)], b1_send.at[0])
    drain_send(bias_out.at[:, pl.ds(0, GROUP - 1)], b2_send.at[0])


def finish(parts, bias, att_out, gq_out, gk_out, gv_out, bias_out, held, in_sems, out_sems):
    outs = (att_out, gq_out, gk_out, gv_out)
    arrive = [pltpu.make_async_copy(parts.at[n], held.at[n], in_sems.at[n]) for n in range(4)]
    leave = [pltpu.make_async_copy(held.at[n], outs[n].at[0], out_sems.at[n]) for n in range(4)]
    for copy in arrive:
        copy.start()
    for n in range(4):
        arrive[n].wait()
        leave[n].start()
    chunks = bias_out.shape[1] // 128
    mirrored = mirror_lanes(bias[...].reshape(PAIRS * GROUP * 16, 128))
    for head in range(HEADS):
        dev, pair, odd = head // (2 * PAIRS), head // 2 % PAIRS, head % 2
        base = (pair * GROUP + dev) * 16 + odd * (chunks + 1)
        for c in range(chunks):
            place = (chunks - 1 - c) * 128
            bias_out[head : head + 1, place : place + 128] = mirrored[base + c : base + c + 1, :]
        bias_out[head : head + 1, chunks * 128 :] = mirrored[base + chunks : base + chunks + 1, :1]
    for copy in leave:
        copy.wait()


def body(queries, keys, values, rel_bias, grad_out):
    rec_dev, frames, width = queries.shape
    n_dp = lax.axis_size("dp")
    n_groups = lax.axis_size("ctx") // GROUP
    n_peer = n_dp * n_groups
    span = (2 * NB + 1) * frames
    ctxw = NB * frames
    own = GROUP * frames
    rows = own + 2 * ctxw
    block = jax.ShapeDtypeStruct(queries.shape, jnp.bfloat16)
    bf16, f32 = jnp.bfloat16, jnp.float32
    dma = pltpu.SemaphoreType.DMA
    anywhere = pl.BlockSpec(memory_space=pl.ANY)
    hbm = pl.BlockSpec(memory_space=pltpu.HBM)
    vmem = pl.BlockSpec(memory_space=pltpu.VMEM)
    macs = 6 * GROUP * frames * span * 2 * PAIRS * HEAD
    parts, bias = pl.pallas_call(
        functools.partial(kernel, n_dp, n_groups, frames),
        out_shape=(
            jax.ShapeDtypeStruct((4, frames, width), bf16),
            jax.ShapeDtypeStruct((PAIRS, GROUP, 16, 128), f32),
        ),
        in_specs=[hbm, hbm, hbm, hbm, vmem],
        out_specs=(anywhere, vmem),
        scratch_shapes=[
            pltpu.VMEM((PAIRS, 2, own, LANES), bf16),
            pltpu.VMEM((PAIRS, 2, rows, LANES), bf16),
            pltpu.VMEM((HEADS, span), f32),
            pltpu.VMEM((PAIRS, 2 * frames, span), f32),
            pltpu.VMEM((PAIRS, 2 * frames, span), f32),
            pltpu.VMEM((PAIRS, LANES, rows), f32),
            pltpu.VMEM((PAIRS, LANES, rows), f32),
            pltpu.VMEM((2, 2 * frames, span), bf16),
            pltpu.VMEM((2, 2 * frames, span), bf16),
            pltpu.VMEM((2, LANES, 2 * frames), bf16),
            pltpu.VMEM((2, LANES, 2 * frames), bf16),
            pltpu.VMEM((PAIRS, 2, NB, 2, LANES, frames), bf16),
            pltpu.VMEM((PAIRS, 2, NB, 2, LANES, frames), bf16),
            pltpu.VMEM((PAIRS, GROUP, 4, frames, LANES), bf16),
            pltpu.VMEM((PAIRS, n_peer, 16, 128), f32),
            pltpu.VMEM((PAIRS, 16, 128), f32),
            dma((4, PAIRS)),
            dma((1,)),
            dma((PAIRS, GROUP)),
            dma((PAIRS,)),
            dma((2,)),
            dma((PAIRS, 2)),
            dma((2,)),
            dma((PAIRS, 2, NB)),
            dma((1,)),
            dma((1,)),
            dma((1,)),
            dma((1,)),
            dma((PAIRS,)),
            dma((1,)),
            dma((PAIRS,)),
        ],
        compiler_params=pltpu.CompilerParams(
            collective_id=0, has_side_effects=True, vmem_limit_bytes=VMEM_LIMIT
        ),
        cost_estimate=pl.CostEstimate(
            flops=2 * macs, bytes_accessed=8 * frames * width * 2, transcendentals=own * span * 2 * PAIRS
        ),
    )(queries, keys, values, grad_out, rel_bias)
    return pl.pallas_call(
        finish,
        out_shape=(block, block, block, block, jax.ShapeDtypeStruct(rel_bias.shape, f32)),
        in_specs=[anywhere, vmem],
        out_specs=(hbm, hbm, hbm, hbm, vmem),
        scratch_shapes=[pltpu.VMEM((4, frames, width), bf16), dma((4,)), dma((4,))],
        compiler_params=pltpu.CompilerParams(vmem_limit_bytes=VMEM_LIMIT),
        cost_estimate=pl.CostEstimate(
            flops=0, bytes_accessed=8 * frames * width * 2, transcendentals=0
        ),
    )(parts, bias)


def solution(mesh):
    placed = (
        P("dp", "ctx", None),
        P("dp", "ctx", None),
        P("dp", "ctx", None),
        P(),
        P("dp", "ctx", None),
    )
    return jax.shard_map(
        body,
        mesh=mesh,
        in_specs=placed,
        out_specs=(
            P("dp", "ctx", None),
            P("dp", "ctx", None),
            P("dp", "ctx", None),
            P("dp", "ctx", None),
            P(),
        ),
        check_vma=False,
    )
```

```python
import functools
import math

import jax
import jax.numpy as jnp
from jax import lax
from jax.experimental import pallas as pl
from jax.experimental.pallas import tpu as pltpu
from jax.sharding import PartitionSpec as P

HEADS = 16
HEAD = 64
NB = 3
GROUP = 4
PAIRS = HEADS // GROUP // 2
LANES = 2 * HEAD
EXCLUDED = -1e30
VMEM_LIMIT = 40 * 1024 * 1024
MESH = pl.DeviceIdType.MESH
Q, K, V, G = 0, 1, 2, 3
NT = (((1,), (1,)), ((), ()))


ORDER = (0, 3, 1, 2)
DONE = {0: ((0, 0),), 3: ((1, 2),), 1: ((0, 1),), 2: ((1, 0), (1, 1), (0, 2))}


def dot(a, b, dims=(((1,), (0,)), ((), ()))):
    return lax.dot_general(a, b, dims, preferred_element_type=jnp.float32)


def mirror_lanes(x):
    row = lax.broadcasted_iota(jnp.int32, (128, 128), 0)
    col = lax.broadcasted_iota(jnp.int32, (128, 128), 1)
    exchange = (row + col == 127).astype(jnp.float32)
    return jnp.dot(
        x, exchange, precision=lax.Precision.HIGHEST, preferred_element_type=jnp.float32
    )


def kernel(
    n_dp, n_groups, frames,
    q_hbm, k_hbm, v_hbm, g_hbm, rel_hbm,
    parts_out, bias_out,
    inbuf, rel_ref, qgbuf, kvbuf, rev_buf, bias_tab, bias_acc, gk_acc, gv_acc,
    ds_buf, w_buf, qt_buf, gt_buf, halo_out, halo_in, ostage, b1buf, sum_buf,
    loc_sem, a_send, kv_recv, qg_recv, h_send, h_recv, g_send, g_recv,
    o_send, o_recv, o_loc, b1_send, b1_recv, b2_send, b2_recv,
):
    span = (2 * NB + 1) * frames
    ctxw = NB * frames
    own = GROUP * frames
    score_scale = 1.0 / math.sqrt(HEAD)
    dp = lax.axis_index("dp")
    ctx = lax.axis_index("ctx")
    g = lax.div(ctx, GROUP)
    i = lax.rem(ctx, GROUP)
    n_peer = n_dp * n_groups
    slot = dp * n_groups + g
    has_lo = g > 0
    has_hi = g < n_groups - 1
    srcs = (q_hbm, k_hbm, v_hbm, g_hbm)
    accs = (gk_acc, gv_acc)

    def group_dev(j):
        return {"dp": dp, "ctx": g * GROUP + j}

    def side_dev(direction):
        return {"dp": dp, "ctx": ctx + (GROUP if direction else -GROUP)}

    def peer_dev(s):
        return {"dp": lax.div(s, n_groups), "ctx": lax.rem(s, n_groups) * GROUP + i}

    def lanes(j, p):
        return pl.ds(pl.multiple_of((j * PAIRS + p) * LANES, LANES), LANES)

    def rows_of(arr, p, j):
        if arr in (K, V):
            start = pl.multiple_of(ctxw + j * frames, frames)
            return kvbuf.at[p, arr - K, pl.ds(start, frames), :]
        start = pl.multiple_of(j * frames, frames)
        return qgbuf.at[p, 0 if arr == Q else 1, pl.ds(start, frames), :]

    def load(arr):
        return pltpu.make_async_copy(srcs[arr].at[0], inbuf.at[arr], loc_sem.at[arr])

    def place_own(arr, p):
        rows_of(arr, p, i)[...] = inbuf[arr, :, lanes(i, p)]

    def remote(src, dst, send_sem, recv_sem, device):
        return pltpu.make_async_remote_copy(
            src_ref=src, dst_ref=dst, send_sem=send_sem, recv_sem=recv_sem,
            device_id=device, device_id_type=MESH,
        )

    def a_copy(arr, p, j):
        recv = kv_recv.at[p, i] if arr in (K, V) else qg_recv.at[p]
        return remote(
            inbuf.at[arr, :, lanes(j, p)], rows_of(arr, p, i), a_send.at[0], recv, group_dev(j)
        )

    def kv_arrival(p, j):
        block = kvbuf.at[p, :, pl.ds(pl.multiple_of(ctxw + j * frames, frames), frames), :]
        return remote(block, block, a_send.at[0], kv_recv.at[p, j], group_dev(j))

    def qg_arrival(p):
        blocks = qgbuf.at[p, :, pl.ds(0, own - frames), :]
        return remote(blocks, blocks, a_send.at[0], qg_recv.at[p], group_dev(i))

    def halo_copy(p, direction, j):
        src = pl.multiple_of(ctxw + j * frames, frames)
        place = j - 1 if direction else j
        dst = pl.multiple_of(place * frames + (0 if direction else ctxw + own), frames)
        return remote(
            kvbuf.at[p, :, pl.ds(src, frames), :],
            kvbuf.at[p, :, pl.ds(dst, frames), :],
            h_send.at[direction], h_recv.at[p, direction], side_dev(direction),
        )

    def halo_arrival(p, direction):
        blocks = kvbuf.at[p, :, pl.ds(0 if direction else ctxw + own, ctxw), :]
        return remote(
            blocks, blocks, h_send.at[direction], h_recv.at[p, direction], side_dev(direction)
        )

    def grad_copy(p, direction, blk):
        return remote(
            halo_out.at[p, direction, blk], halo_in.at[p, direction, blk],
            g_send.at[direction], g_recv.at[p, direction, blk], side_dev(direction),
        )

    def out_parts(half, p, j):
        return ostage.at[p, j, pl.ds(2 * half, 2)]

    def out_copy(half, p, j):
        return remote(
            out_parts(half, p, j), parts_out.at[pl.ds(2 * half, 2), :, lanes(i, p)],
            o_send.at[0], o_recv.at[0], group_dev(j),
        )

    def send_out(half, p, j):
        @pl.when(j != i)
        def _():
            out_copy(half, p, j).start()

        @pl.when(j == i)
        def _():
            pltpu.make_async_copy(
                out_parts(half, p, j), parts_out.at[pl.ds(2 * half, 2), :, lanes(i, p)], o_loc.at[0]
            ).start()

    def b1_copy(p, s):
        return remote(
            b1buf.at[p, slot], b1buf.at[p, slot], b1_send.at[0], b1_recv.at[p], peer_dev(s)
        )

    def b2_copy(p, j):
        return remote(sum_buf.at[p], bias_out.at[p, i], b2_send.at[0], b2_recv.at[p], group_dev(j))

    def others(fn):
        core = lax.rem(i, 2)
        far = 2 - 2 * lax.div(i, 2)
        fn(i + 1 - 2 * core)
        fn(far + core)
        fn(far + 1 - core)

    def all_peers(fn):
        def step(t, carry):
            fn(lax.rem(slot + t, n_peer))
            return carry

        lax.fori_loop(1, n_peer, step, 0)

    barrier = pltpu.get_barrier_semaphore()

    def greet(device):
        pl.semaphore_signal(barrier, inc=1, device_id=device, device_id_type=MESH)

    others(lambda j: greet(group_dev(j)))
    all_peers(lambda s: greet(peer_dev(s)))
    load_rel = pltpu.make_async_copy(rel_hbm, rel_ref, loc_sem.at[4])
    for arr in (K, V, Q, G):
        load(arr).start()
    load_rel.start()

    bias_acc[...] = jnp.zeros_like(bias_acc)
    gk_acc[...] = jnp.zeros_like(gk_acc)
    gv_acc[...] = jnp.zeros_like(gv_acc)
    edge_zero = jnp.zeros((PAIRS, 2, ctxw, LANES), jnp.bfloat16)
    edge_grad = jnp.zeros((PAIRS, NB, 2, LANES, frames), jnp.bfloat16)

    @pl.when(jnp.logical_not(has_lo))
    def _():
        kvbuf[:, :, :ctxw, :] = edge_zero
        halo_in[:, 1] = edge_grad

    @pl.when(jnp.logical_not(has_hi))
    def _():
        kvbuf[:, :, ctxw + own :, :] = edge_zero
        halo_in[:, 0] = edge_grad

    pl.semaphore_wait(barrier, GROUP - 1 + n_peer - 1)

    def send_inputs(p):
        for arr in (K, V, Q, G):
            others(lambda j: a_copy(arr, p, j).start())

    for arr in (K, V, Q, G):
        load(arr).wait()
    send_inputs(0)
    for arr in (K, V, Q, G):
        for p in range(PAIRS):
            place_own(arr, p)
    load_rel.wait()

    chunks = 2 * ctxw // 128
    for c in range(chunks):
        rev_buf[:, (chunks - 1 - c) * 128 : (chunks - c) * 128] = mirror_lanes(
            rel_ref[:, c * 128 : (c + 1) * 128]
        )
    last_lane = lax.broadcasted_iota(jnp.int32, (HEADS, 128), 1) == 127
    rev_buf[:, 2 * ctxw :] = jnp.where(
        last_lane, rel_ref[:, 2 * ctxw : 2 * ctxw + 1], jnp.float32(EXCLUDED)
    )
    for p in range(PAIRS):
        for h in range(2):
            row = rev_buf[pl.ds(i * (2 * PAIRS) + 2 * p + h, 1), :]
            table = jnp.broadcast_to(row, (frames, span))
            bias_tab[p, h * frames : (h + 1) * frames, :] = pltpu.roll(
                table, 1, 1, stride=1, stride_axis=0
            )
    def forward_halo(p):
        def forward(j):
            @pl.when(has_lo & (j < NB))
            def _():
                halo_copy(p, 0, j).start()

            @pl.when(has_hi & (j > 0))
            def _():
                halo_copy(p, 1, j).start()

        forward(i)

        def passed_on(j):
            kv_arrival(p, j).wait_recv()
            forward(j)

        others(passed_on)

    def wait_inputs(p):
        qg_arrival(p).wait_recv()

        @pl.when(has_lo)
        def _():
            halo_arrival(p, 1).wait_recv()

        @pl.when(has_hi)
        def _():
            halo_arrival(p, 0).wait_recv()

    low = lax.broadcasted_iota(jnp.int32, (frames, LANES), 1) < HEAD

    def stack_heads(x):
        zero = jnp.zeros_like(x)
        return jnp.concatenate([jnp.where(low, x, zero), jnp.where(low, zero, x)], axis=0)

    def merge_heads(x):
        return jnp.where(low, x[:frames], x[frames:])

    column = lax.broadcasted_iota(jnp.int32, (1, span), 1)

    top_half = lax.broadcasted_iota(jnp.int32, (LANES, frames), 0) < HEAD

    def stack_turned(x):
        turned = x.T
        zero = jnp.zeros_like(turned)
        return jnp.concatenate(
            [jnp.where(top_half, turned, zero), jnp.where(top_half, zero, turned)], axis=1
        ).astype(jnp.bfloat16)

    def softmax_part(n, p, b):
        own_rows = slice(b * frames, (b + 1) * frames)
        window = slice(b * frames, b * frames + span)
        key_row = column + ((g * GROUP - NB + b) * frames)
        exists = (key_row >= 0) & (key_row < n_groups * own)
        edge = jnp.where(exists, 0.0, EXCLUDED).astype(jnp.float32)
        kw = kvbuf[p, 0, window, :]
        vw = kvbuf[p, 1, window, :]
        q32 = qgbuf[p, 0, own_rows, :].astype(jnp.float32) * score_scale
        g32 = qgbuf[p, 1, own_rows, :].astype(jnp.float32)
        qs = stack_heads(q32).astype(jnp.bfloat16)
        gs32 = stack_heads(g32)
        gs = gs32.astype(jnp.bfloat16)
        qt_buf[n % 2] = stack_turned(q32)
        gt_buf[n % 2] = stack_turned(g32)
        scores = dot(qs, kw, NT) + bias_tab[p] + edge
        top = jnp.max(scores, axis=1, keepdims=True)
        expd = jnp.exp(scores - top)
        total = jnp.sum(expd, axis=1, keepdims=True)
        probs = expd * (1.0 / total)
        weights = probs.astype(jnp.bfloat16)
        w_buf[n % 2] = weights
        attended = merge_heads(dot(weights, vw)).astype(jnp.bfloat16)
        ostage[p, b, 0] = attended
        wide = attended.astype(jnp.float32)
        delta = jnp.sum(gs32 * jnp.concatenate([wide, wide], axis=0), axis=1, keepdims=True)
        dscore = probs * (dot(gs, vw, NT) - delta)
        ds_buf[n % 2] = dscore.astype(jnp.bfloat16)
        bias_acc[p] += dscore

    def grad_part(n, p, b):
        window = slice(b * frames, b * frames + span)
        dscore_low = ds_buf[n % 2]
        grad_q = merge_heads(dot(dscore_low, kvbuf[p, 0, window, :])) * score_scale
        ostage[p, b, 1] = grad_q.astype(jnp.bfloat16)
        gk_acc[p, :, window] += dot(qt_buf[n % 2], dscore_low)
        gv_acc[p, :, window] += dot(gt_buf[n % 2], w_buf[n % 2])

    def send_grads(p, b):
        send_out(0, p, b)
        for direction, blk in DONE[b]:
            start = blk * frames + (ctxw + own if direction else 0)

            @pl.when(has_hi if direction else has_lo)
            def _():
                for a in range(2):
                    halo_out[p, direction, blk, a] = accs[a][p, :, start : start + frames].astype(
                        jnp.bfloat16
                    )
                grad_copy(p, direction, blk).start()

    def send_bias(p):
        sub = lax.broadcasted_iota(jnp.int32, (8, span), 0)
        b1buf[p, slot] = jnp.zeros((16, 128), jnp.float32)
        for h in range(2):
            part = bias_acc[p, h * frames : (h + 1) * frames, :]
            rows = frames
            while rows > 8:
                rows //= 2
                part = part[:rows] + pltpu.roll(part[rows:], span - rows, 1)
            for s in (4, 2, 1):
                part = jnp.where((sub & s) != 0, pltpu.roll(part, span - s, 1), part)
            diag = pltpu.roll(jnp.sum(part, axis=0, keepdims=True), span - 1, 1)
            for c in range(span // 128):
                n = h * (span // 128) + c
                b1buf[p, slot, n : n + 1, :] = diag[:, c * 128 : (c + 1) * 128]
        all_peers(lambda s: b1_copy(p, s).start())

    def sum_bias(p):
        others_part = b1buf.at[p, pl.ds(0, n_peer - 1)]
        remote(
            others_part, others_part, b1_send.at[0], b1_recv.at[p], group_dev(i)
        ).wait_recv()
        sum_buf[p] = lax.fori_loop(
            0, n_peer, lambda s, acc: acc + b1buf[p, s], jnp.zeros((16, 128), jnp.float32)
        )
        others(lambda j: b2_copy(p, j).start())
        bias_out[p, i] = sum_buf[p]

    def finish_grads(p):
        for j in (2, 0, 1, 3):
            if j < NB:
                @pl.when(has_lo)
                def _():
                    grad_copy(p, 1, j).wait_recv()
            if j > 0:
                @pl.when(has_hi)
                def _():
                    grad_copy(p, 0, j - 1).wait_recv()
            start = ctxw + j * frames
            for a in range(2):
                full = accs[a][p, :, start : start + frames]
                if j < NB:
                    full = full + halo_in[p, 1, j, a].astype(jnp.float32)
                if j > 0:
                    full = full + halo_in[p, 0, j - 1, a].astype(jnp.float32)
                ostage[p, j, 2 + a] = full.T.astype(jnp.bfloat16)
            send_out(1, p, j)

    units = [(p, b) for p in range(PAIRS) for b in ORDER]
    forward_halo(0)
    for p in range(1, PAIRS):
        send_inputs(p)
    for n, (p, b) in enumerate(units):
        if b == ORDER[0]:
            wait_inputs(p)
        softmax_part(n, p, b)
        if n > 0:
            grad_part(n - 1, *units[n - 1])
            send_grads(*units[n - 1])
        if b == ORDER[0]:
            if p + 1 < PAIRS:
                forward_halo(p + 1)
            if p > 0:
                send_bias(p - 1)
        if b == ORDER[2] and p > 0:
            sum_bias(p - 1)
            finish_grads(p - 1)
    grad_part(len(units) - 1, *units[-1])
    send_grads(*units[-1])
    send_bias(PAIRS - 1)
    finish_grads(PAIRS - 1)
    sum_bias(PAIRS - 1)

    def drain_send(ref, sem):
        remote(ref, ref, sem, sem, group_dev(i)).wait_send()

    def drain_recv(ref, sem):
        remote(ref, ref, sem, sem, group_dev(i)).wait_recv()

    for p in range(PAIRS):
        drain_recv(bias_out.at[p, pl.ds(0, GROUP - 1)], b2_recv.at[p])
    mine = PAIRS * LANES
    drain_recv(parts_out.at[:, :, pl.ds(0, (GROUP - 1) * mine)], o_recv.at[0])
    own_part = parts_out.at[:, :, pl.ds(0, mine)]
    pltpu.make_async_copy(own_part, own_part, o_loc.at[0]).wait()
    drain_send(parts_out.at[:, :, pl.ds(0, (GROUP - 1) * mine)], o_send.at[0])
    drain_send(parts_out.at[:, :, pl.ds(0, (GROUP - 1) * mine)], a_send.at[0])
    for direction, exists in ((0, has_lo), (1, has_hi)):
        @pl.when(exists)
        def _():
            drain_send(kvbuf.at[:, :, pl.ds(0, ctxw), :], h_send.at[direction])
            drain_send(halo_out.at[:, direction], g_send.at[direction])

    drain_send(b1buf.at[:, pl.ds(0, n_peer - 1)], b1_send.at[0])
    drain_send(bias_out.at[:, pl.ds(0, GROUP - 1)], b2_send.at[0])


def finish(parts, bias, att_out, gq_out, gk_out, gv_out, bias_out, sems):
    outs = (att_out, gq_out, gk_out, gv_out)
    leave = [pltpu.make_async_copy(parts.at[n], outs[n].at[0], sems.at[n]) for n in range(4)]
    for copy in leave:
        copy.start()
    chunks = bias_out.shape[1] // 128
    mirrored = mirror_lanes(bias[...].reshape(PAIRS * GROUP * 16, 128))
    for head in range(HEADS):
        dev, pair, odd = head // (2 * PAIRS), head // 2 % PAIRS, head % 2
        base = (pair * GROUP + dev) * 16 + odd * (chunks + 1)
        for c in range(chunks):
            place = (chunks - 1 - c) * 128
            bias_out[head : head + 1, place : place + 128] = mirrored[base + c : base + c + 1, :]
        bias_out[head : head + 1, chunks * 128 :] = mirrored[base + chunks : base + chunks + 1, :1]
    for copy in leave:
        copy.wait()


def body(queries, keys, values, rel_bias, grad_out):
    rec_dev, frames, width = queries.shape
    n_dp = lax.axis_size("dp")
    n_groups = lax.axis_size("ctx") // GROUP
    n_peer = n_dp * n_groups
    span = (2 * NB + 1) * frames
    ctxw = NB * frames
    own = GROUP * frames
    rows = own + 2 * ctxw
    block = jax.ShapeDtypeStruct(queries.shape, jnp.bfloat16)
    bf16, f32 = jnp.bfloat16, jnp.float32
    dma = pltpu.SemaphoreType.DMA
    anywhere = pl.BlockSpec(memory_space=pl.ANY)
    hbm = pl.BlockSpec(memory_space=pltpu.HBM)
    vmem = pl.BlockSpec(memory_space=pltpu.VMEM)
    macs = 6 * GROUP * frames * span * 2 * PAIRS * HEAD
    operands = (queries, keys, values, grad_out, rel_bias)
    parts, bias = pl.pallas_call(
        functools.partial(kernel, n_dp, n_groups, frames),
        out_shape=(
            jax.ShapeDtypeStruct((4, frames, width), bf16),
            jax.ShapeDtypeStruct((PAIRS, GROUP, 16, 128), f32),
        ),
        in_specs=[hbm, hbm, hbm, hbm, hbm],
        out_specs=(anywhere, vmem),
        scratch_shapes=[
            pltpu.VMEM((4, frames, width), bf16),
            pltpu.VMEM(rel_bias.shape, f32),
            pltpu.VMEM((PAIRS, 2, own, LANES), bf16),
            pltpu.VMEM((PAIRS, 2, rows, LANES), bf16),
            pltpu.VMEM((HEADS, span), f32),
            pltpu.VMEM((PAIRS, 2 * frames, span), f32),
            pltpu.VMEM((PAIRS, 2 * frames, span), f32),
            pltpu.VMEM((PAIRS, LANES, rows), f32),
            pltpu.VMEM((PAIRS, LANES, rows), f32),
            pltpu.VMEM((2, 2 * frames, span), bf16),
            pltpu.VMEM((2, 2 * frames, span), bf16),
            pltpu.VMEM((2, LANES, 2 * frames), bf16),
            pltpu.VMEM((2, LANES, 2 * frames), bf16),
            pltpu.VMEM((PAIRS, 2, NB, 2, LANES, frames), bf16),
            pltpu.VMEM((PAIRS, 2, NB, 2, LANES, frames), bf16),
            pltpu.VMEM((PAIRS, GROUP, 4, frames, LANES), bf16),
            pltpu.VMEM((PAIRS, n_peer, 16, 128), f32),
            pltpu.VMEM((PAIRS, 16, 128), f32),
            dma((5,)),
            dma((1,)),
            dma((PAIRS, GROUP)),
            dma((PAIRS,)),
            dma((2,)),
            dma((PAIRS, 2)),
            dma((2,)),
            dma((PAIRS, 2, NB)),
            dma((1,)),
            dma((1,)),
            dma((1,)),
            dma((1,)),
            dma((PAIRS,)),
            dma((1,)),
            dma((PAIRS,)),
        ],
        compiler_params=pltpu.CompilerParams(
            collective_id=0, has_side_effects=True, vmem_limit_bytes=VMEM_LIMIT
        ),
        cost_estimate=pl.CostEstimate(
            flops=2 * macs, bytes_accessed=8 * frames * width * 2, transcendentals=own * span * 2 * PAIRS
        ),
    )(*(pltpu.with_memory_space_constraint(x, pltpu.HBM) for x in operands))
    return pl.pallas_call(
        finish,
        out_shape=(block, block, block, block, jax.ShapeDtypeStruct(rel_bias.shape, f32)),
        in_specs=[vmem, vmem],
        out_specs=(hbm, hbm, hbm, hbm, vmem),
        scratch_shapes=[dma((4,))],
        compiler_params=pltpu.CompilerParams(vmem_limit_bytes=VMEM_LIMIT),
        cost_estimate=pl.CostEstimate(
            flops=0, bytes_accessed=8 * frames * width * 2, transcendentals=0
        ),
    )(parts, bias)


def solution(mesh):
    placed = (
        P("dp", "ctx", None),
        P("dp", "ctx", None),
        P("dp", "ctx", None),
        P(),
        P("dp", "ctx", None),
    )
    return jax.shard_map(
        body,
        mesh=mesh,
        in_specs=placed,
        out_specs=(
            P("dp", "ctx", None),
            P("dp", "ctx", None),
            P("dp", "ctx", None),
            P("dp", "ctx", None),
            P(),
        ),
        check_vma=False,
    )
```

```python
import functools
import math

import jax
import jax.numpy as jnp
from jax import lax
from jax.experimental import pallas as pl
from jax.experimental.pallas import tpu as pltpu
from jax.sharding import PartitionSpec as P

HEADS = 16
HEAD = 64
NB = 3
GROUP = 4
PAIRS = HEADS // GROUP // 2
LANES = 2 * HEAD
EXCLUDED = -1e30
VMEM_LIMIT = 40 * 1024 * 1024
MESH = pl.DeviceIdType.MESH
Q, K, V, G = 0, 1, 2, 3
STRIP = 16
NT = (((1,), (1,)), ((), ()))


ORDER = (0, 3, 1, 2)
DONE = {0: ((0, 0),), 3: ((1, 2),), 1: ((0, 1),), 2: ((1, 0), (1, 1), (0, 2))}


def dot(a, b, dims=(((1,), (0,)), ((), ()))):
    return lax.dot_general(a, b, dims, preferred_element_type=jnp.float32)


def mirror_lanes(x):
    row = lax.broadcasted_iota(jnp.int32, (128, 128), 0)
    col = lax.broadcasted_iota(jnp.int32, (128, 128), 1)
    exchange = (row + col == 127).astype(jnp.float32)
    return jnp.dot(
        x, exchange, precision=lax.Precision.HIGHEST, preferred_element_type=jnp.float32
    )


def kernel(
    n_dp, n_groups, frames,
    q_hbm, k_hbm, v_hbm, g_hbm, rel_hbm,
    parts_out, bias_out,
    inbuf, rel_ref, qgbuf, kvbuf, rev_buf, bias_tab, bias_acc, gk_acc, gv_acc,
    score_buf, prob_buf, dprob_buf, ds_buf, w_buf, qt_buf, gt_buf, halo_out, halo_in, ostage, b1buf, sum_buf,
    loc_sem, a_send, kv_recv, qg_recv, h_send, h_recv, g_send, g_recv,
    o_send, o_recv, o_loc, b1_send, b1_recv, b2_send, b2_recv,
):
    span = (2 * NB + 1) * frames
    ctxw = NB * frames
    own = GROUP * frames
    score_scale = 1.0 / math.sqrt(HEAD)
    dp = lax.axis_index("dp")
    ctx = lax.axis_index("ctx")
    g = lax.div(ctx, GROUP)
    i = lax.rem(ctx, GROUP)
    n_peer = n_dp * n_groups
    slot = dp * n_groups + g
    has_lo = g > 0
    has_hi = g < n_groups - 1
    srcs = (q_hbm, k_hbm, v_hbm, g_hbm)
    accs = (gk_acc, gv_acc)

    def group_dev(j):
        return {"dp": dp, "ctx": g * GROUP + j}

    def side_dev(direction):
        return {"dp": dp, "ctx": ctx + (GROUP if direction else -GROUP)}

    def peer_dev(s):
        return {"dp": lax.div(s, n_groups), "ctx": lax.rem(s, n_groups) * GROUP + i}

    def lanes(j, p):
        return pl.ds(pl.multiple_of((j * PAIRS + p) * LANES, LANES), LANES)

    def rows_of(arr, p, j):
        if arr in (K, V):
            start = pl.multiple_of(ctxw + j * frames, frames)
            return kvbuf.at[p, arr - K, pl.ds(start, frames), :]
        start = pl.multiple_of(j * frames, frames)
        return qgbuf.at[p, 0 if arr == Q else 1, pl.ds(start, frames), :]

    def load(arr):
        return pltpu.make_async_copy(srcs[arr].at[0], inbuf.at[arr], loc_sem.at[arr])

    def place_own(arr, p):
        rows_of(arr, p, i)[...] = inbuf[arr, :, lanes(i, p)]

    def remote(src, dst, send_sem, recv_sem, device):
        return pltpu.make_async_remote_copy(
            src_ref=src, dst_ref=dst, send_sem=send_sem, recv_sem=recv_sem,
            device_id=device, device_id_type=MESH,
        )

    def a_copy(arr, p, j):
        recv = kv_recv.at[p, i] if arr in (K, V) else qg_recv.at[p]
        return remote(
            inbuf.at[arr, :, lanes(j, p)], rows_of(arr, p, i), a_send.at[0], recv, group_dev(j)
        )

    def kv_arrival(p, j):
        block = kvbuf.at[p, :, pl.ds(pl.multiple_of(ctxw + j * frames, frames), frames), :]
        return remote(block, block, a_send.at[0], kv_recv.at[p, j], group_dev(j))

    def qg_arrival(p):
        blocks = qgbuf.at[p, :, pl.ds(0, own - frames), :]
        return remote(blocks, blocks, a_send.at[0], qg_recv.at[p], group_dev(i))

    def halo_copy(p, direction, j):
        src = pl.multiple_of(ctxw + j * frames, frames)
        place = j - 1 if direction else j
        dst = pl.multiple_of(place * frames + (0 if direction else ctxw + own), frames)
        return remote(
            kvbuf.at[p, :, pl.ds(src, frames), :],
            kvbuf.at[p, :, pl.ds(dst, frames), :],
            h_send.at[direction], h_recv.at[p, direction], side_dev(direction),
        )

    def halo_arrival(p, direction):
        blocks = kvbuf.at[p, :, pl.ds(0 if direction else ctxw + own, ctxw), :]
        return remote(
            blocks, blocks, h_send.at[direction], h_recv.at[p, direction], side_dev(direction)
        )

    def grad_copy(p, direction, blk):
        return remote(
            halo_out.at[p, direction, blk], halo_in.at[p, direction, blk],
            g_send.at[direction], g_recv.at[p, direction, blk], side_dev(direction),
        )

    def out_parts(half, p, j):
        return ostage.at[p, j, pl.ds(2 * half, 2)]

    def out_copy(half, p, j):
        return remote(
            out_parts(half, p, j), parts_out.at[pl.ds(2 * half, 2), :, lanes(i, p)],
            o_send.at[0], o_recv.at[0], group_dev(j),
        )

    def send_out(half, p, j):
        @pl.when(j != i)
        def _():
            out_copy(half, p, j).start()

        @pl.when(j == i)
        def _():
            pltpu.make_async_copy(
                out_parts(half, p, j), parts_out.at[pl.ds(2 * half, 2), :, lanes(i, p)], o_loc.at[0]
            ).start()

    def b1_copy(p, s):
        return remote(
            b1buf.at[p, slot], b1buf.at[p, slot], b1_send.at[0], b1_recv.at[p], peer_dev(s)
        )

    def b2_copy(p, j):
        return remote(sum_buf.at[p], bias_out.at[p, i], b2_send.at[0], b2_recv.at[p], group_dev(j))

    def others(fn):
        core = lax.rem(i, 2)
        far = 2 - 2 * lax.div(i, 2)
        fn(i + 1 - 2 * core)
        fn(far + core)
        fn(far + 1 - core)

    def all_peers(fn):
        def step(t, carry):
            fn(lax.rem(slot + t, n_peer))
            return carry

        lax.fori_loop(1, n_peer, step, 0)

    barrier = pltpu.get_barrier_semaphore()

    def greet(device):
        pl.semaphore_signal(barrier, inc=1, device_id=device, device_id_type=MESH)

    others(lambda j: greet(group_dev(j)))
    all_peers(lambda s: greet(peer_dev(s)))
    load_rel = pltpu.make_async_copy(rel_hbm, rel_ref, loc_sem.at[4])
    for arr in (K, V, Q, G):
        load(arr).start()
    load_rel.start()

    bias_acc[...] = jnp.zeros_like(bias_acc)
    gk_acc[...] = jnp.zeros_like(gk_acc)
    gv_acc[...] = jnp.zeros_like(gv_acc)
    edge_zero = jnp.zeros((PAIRS, 2, ctxw, LANES), jnp.bfloat16)
    edge_grad = jnp.zeros((PAIRS, NB, 2, LANES, frames), jnp.bfloat16)

    @pl.when(jnp.logical_not(has_lo))
    def _():
        kvbuf[:, :, :ctxw, :] = edge_zero
        halo_in[:, 1] = edge_grad

    @pl.when(jnp.logical_not(has_hi))
    def _():
        kvbuf[:, :, ctxw + own :, :] = edge_zero
        halo_in[:, 0] = edge_grad

    pl.semaphore_wait(barrier, GROUP - 1 + n_peer - 1)

    def send_inputs(p):
        for arr in (K, V, Q, G):
            others(lambda j: a_copy(arr, p, j).start())

    for arr in (K, V, Q, G):
        load(arr).wait()
    send_inputs(0)
    for arr in (K, V, Q, G):
        for p in range(PAIRS):
            place_own(arr, p)
    load_rel.wait()

    chunks = 2 * ctxw // 128
    for c in range(chunks):
        rev_buf[:, (chunks - 1 - c) * 128 : (chunks - c) * 128] = mirror_lanes(
            rel_ref[:, c * 128 : (c + 1) * 128]
        )
    last_lane = lax.broadcasted_iota(jnp.int32, (HEADS, 128), 1) == 127
    rev_buf[:, 2 * ctxw :] = jnp.where(
        last_lane, rel_ref[:, 2 * ctxw : 2 * ctxw + 1], jnp.float32(EXCLUDED)
    )
    for p in range(PAIRS):
        for h in range(2):
            row = rev_buf[pl.ds(i * (2 * PAIRS) + 2 * p + h, 1), :]
            table = jnp.broadcast_to(row, (frames, span))
            bias_tab[p, h * frames : (h + 1) * frames, :] = pltpu.roll(
                table, 1, 1, stride=1, stride_axis=0
            )
    def forward_halo(p):
        def forward(j):
            @pl.when(has_lo & (j < NB))
            def _():
                halo_copy(p, 0, j).start()

            @pl.when(has_hi & (j > 0))
            def _():
                halo_copy(p, 1, j).start()

        forward(i)

        def passed_on(j):
            kv_arrival(p, j).wait_recv()
            forward(j)

        others(passed_on)

    def wait_inputs(p):
        qg_arrival(p).wait_recv()

        @pl.when(has_lo)
        def _():
            halo_arrival(p, 1).wait_recv()

        @pl.when(has_hi)
        def _():
            halo_arrival(p, 0).wait_recv()

    low = lax.broadcasted_iota(jnp.int32, (frames, LANES), 1) < HEAD

    def stack_heads(x):
        zero = jnp.zeros_like(x)
        return jnp.concatenate([jnp.where(low, x, zero), jnp.where(low, zero, x)], axis=0)

    def merge_heads(x):
        return jnp.where(low, x[:frames], x[frames:])

    column = lax.broadcasted_iota(jnp.int32, (1, span), 1)

    top_half = lax.broadcasted_iota(jnp.int32, (LANES, frames), 0) < HEAD

    def stack_turned(x):
        turned = x.T
        zero = jnp.zeros_like(turned)
        return jnp.concatenate(
            [jnp.where(top_half, turned, zero), jnp.where(top_half, zero, turned)], axis=1
        ).astype(jnp.bfloat16)

    def softmax_part(n, p, b):
        own_rows = slice(b * frames, (b + 1) * frames)
        window = slice(b * frames, b * frames + span)
        key_row = column + ((g * GROUP - NB + b) * frames)
        exists = (key_row >= 0) & (key_row < n_groups * own)
        edge = jnp.where(exists, 0.0, EXCLUDED).astype(jnp.float32)
        kw = kvbuf[p, 0, window, :]
        vw = kvbuf[p, 1, window, :]
        q32 = qgbuf[p, 0, own_rows, :].astype(jnp.float32) * score_scale
        g32 = qgbuf[p, 1, own_rows, :].astype(jnp.float32)
        qs = stack_heads(q32).astype(jnp.bfloat16)
        gs32 = stack_heads(g32)
        gs = gs32.astype(jnp.bfloat16)
        qt_buf[n % 2] = stack_turned(q32)
        gt_buf[n % 2] = stack_turned(g32)
        m = n % 2
        score_buf[m] = dot(qs, kw, NT)
        dprob_buf[m] = dot(gs, vw, NT)
        for r in range(0, 2 * frames, STRIP):
            strip = slice(r, r + STRIP)
            scores = score_buf[m, strip, :] + bias_tab[p, strip, :] + edge
            top = jnp.max(scores, axis=1, keepdims=True)
            expd = jnp.exp(scores - top)
            total = jnp.sum(expd, axis=1, keepdims=True)
            probs = expd * (1.0 / total)
            prob_buf[m, strip, :] = probs
            w_buf[m, strip, :] = probs.astype(jnp.bfloat16)
        weights = w_buf[m]
        attended = merge_heads(dot(weights, vw)).astype(jnp.bfloat16)
        ostage[p, b, 0] = attended
        wide = attended.astype(jnp.float32)
        delta = jnp.sum(gs32 * jnp.concatenate([wide, wide], axis=0), axis=1, keepdims=True)
        for r in range(0, 2 * frames, STRIP):
            strip = slice(r, r + STRIP)
            dscore = prob_buf[m, strip, :] * (dprob_buf[m, strip, :] - delta[strip])
            ds_buf[m, strip, :] = dscore.astype(jnp.bfloat16)
            bias_acc[p, strip, :] += dscore

    def grad_part(n, p, b):
        window = slice(b * frames, b * frames + span)
        dscore_low = ds_buf[n % 2]
        grad_q = merge_heads(dot(dscore_low, kvbuf[p, 0, window, :])) * score_scale
        ostage[p, b, 1] = grad_q.astype(jnp.bfloat16)
        gk_acc[p, :, window] += dot(qt_buf[n % 2], dscore_low)
        gv_acc[p, :, window] += dot(gt_buf[n % 2], w_buf[n % 2])

    def send_grads(p, b):
        send_out(0, p, b)
        for direction, blk in DONE[b]:
            start = blk * frames + (ctxw + own if direction else 0)

            @pl.when(has_hi if direction else has_lo)
            def _():
                for a in range(2):
                    halo_out[p, direction, blk, a] = accs[a][p, :, start : start + frames].astype(
                        jnp.bfloat16
                    )
                grad_copy(p, direction, blk).start()

    def send_bias(p):
        sub = lax.broadcasted_iota(jnp.int32, (8, span), 0)
        b1buf[p, slot] = jnp.zeros((16, 128), jnp.float32)
        for h in range(2):
            part = bias_acc[p, h * frames : (h + 1) * frames, :]
            rows = frames
            while rows > 8:
                rows //= 2
                part = part[:rows] + pltpu.roll(part[rows:], span - rows, 1)
            for s in (4, 2, 1):
                part = jnp.where((sub & s) != 0, pltpu.roll(part, span - s, 1), part)
            diag = pltpu.roll(jnp.sum(part, axis=0, keepdims=True), span - 1, 1)
            for c in range(span // 128):
                n = h * (span // 128) + c
                b1buf[p, slot, n : n + 1, :] = diag[:, c * 128 : (c + 1) * 128]
        all_peers(lambda s: b1_copy(p, s).start())

    def sum_bias(p):
        others_part = b1buf.at[p, pl.ds(0, n_peer - 1)]
        remote(
            others_part, others_part, b1_send.at[0], b1_recv.at[p], group_dev(i)
        ).wait_recv()
        sum_buf[p] = lax.fori_loop(
            0, n_peer, lambda s, acc: acc + b1buf[p, s], jnp.zeros((16, 128), jnp.float32)
        )
        others(lambda j: b2_copy(p, j).start())
        bias_out[p, i] = sum_buf[p]

    def finish_grads(p):
        for j in (2, 0, 1, 3):
            if j < NB:
                @pl.when(has_lo)
                def _():
                    grad_copy(p, 1, j).wait_recv()
            if j > 0:
                @pl.when(has_hi)
                def _():
                    grad_copy(p, 0, j - 1).wait_recv()
            start = ctxw + j * frames
            for a in range(2):
                full = accs[a][p, :, start : start + frames]
                if j < NB:
                    full = full + halo_in[p, 1, j, a].astype(jnp.float32)
                if j > 0:
                    full = full + halo_in[p, 0, j - 1, a].astype(jnp.float32)
                ostage[p, j, 2 + a] = full.T.astype(jnp.bfloat16)
            send_out(1, p, j)

    units = [(p, b) for p in range(PAIRS) for b in ORDER]
    forward_halo(0)
    for p in range(1, PAIRS):
        send_inputs(p)
    for n, (p, b) in enumerate(units):
        if b == ORDER[0]:
            wait_inputs(p)
        softmax_part(n, p, b)
        if n > 0:
            grad_part(n - 1, *units[n - 1])
            send_grads(*units[n - 1])
        if b == ORDER[0]:
            if p + 1 < PAIRS:
                forward_halo(p + 1)
            if p > 0:
                send_bias(p - 1)
        if b == ORDER[2] and p > 0:
            sum_bias(p - 1)
            finish_grads(p - 1)
    grad_part(len(units) - 1, *units[-1])
    send_grads(*units[-1])
    send_bias(PAIRS - 1)
    finish_grads(PAIRS - 1)
    sum_bias(PAIRS - 1)

    def drain_send(ref, sem):
        remote(ref, ref, sem, sem, group_dev(i)).wait_send()

    def drain_recv(ref, sem):
        remote(ref, ref, sem, sem, group_dev(i)).wait_recv()

    for p in range(PAIRS):
        drain_recv(bias_out.at[p, pl.ds(0, GROUP - 1)], b2_recv.at[p])
    mine = PAIRS * LANES
    drain_recv(parts_out.at[:, :, pl.ds(0, (GROUP - 1) * mine)], o_recv.at[0])
    own_part = parts_out.at[:, :, pl.ds(0, mine)]
    pltpu.make_async_copy(own_part, own_part, o_loc.at[0]).wait()
    drain_send(parts_out.at[:, :, pl.ds(0, (GROUP - 1) * mine)], o_send.at[0])
    drain_send(parts_out.at[:, :, pl.ds(0, (GROUP - 1) * mine)], a_send.at[0])
    for direction, exists in ((0, has_lo), (1, has_hi)):
        @pl.when(exists)
        def _():
            drain_send(kvbuf.at[:, :, pl.ds(0, ctxw), :], h_send.at[direction])
            drain_send(halo_out.at[:, direction], g_send.at[direction])

    drain_send(b1buf.at[:, pl.ds(0, n_peer - 1)], b1_send.at[0])
    drain_send(bias_out.at[:, pl.ds(0, GROUP - 1)], b2_send.at[0])


def finish(parts, bias, att_out, gq_out, gk_out, gv_out, bias_out, sems):
    outs = (att_out, gq_out, gk_out, gv_out)
    leave = [pltpu.make_async_copy(parts.at[n], outs[n].at[0], sems.at[n]) for n in range(4)]
    for copy in leave:
        copy.start()
    chunks = bias_out.shape[1] // 128
    mirrored = mirror_lanes(bias[...].reshape(PAIRS * GROUP * 16, 128))
    for head in range(HEADS):
        dev, pair, odd = head // (2 * PAIRS), head // 2 % PAIRS, head % 2
        base = (pair * GROUP + dev) * 16 + odd * (chunks + 1)
        for c in range(chunks):
            place = (chunks - 1 - c) * 128
            bias_out[head : head + 1, place : place + 128] = mirrored[base + c : base + c + 1, :]
        bias_out[head : head + 1, chunks * 128 :] = mirrored[base + chunks : base + chunks + 1, :1]
    for copy in leave:
        copy.wait()


def body(queries, keys, values, rel_bias, grad_out):
    rec_dev, frames, width = queries.shape
    n_dp = lax.axis_size("dp")
    n_groups = lax.axis_size("ctx") // GROUP
    n_peer = n_dp * n_groups
    span = (2 * NB + 1) * frames
    ctxw = NB * frames
    own = GROUP * frames
    rows = own + 2 * ctxw
    block = jax.ShapeDtypeStruct(queries.shape, jnp.bfloat16)
    bf16, f32 = jnp.bfloat16, jnp.float32
    dma = pltpu.SemaphoreType.DMA
    anywhere = pl.BlockSpec(memory_space=pl.ANY)
    hbm = pl.BlockSpec(memory_space=pltpu.HBM)
    vmem = pl.BlockSpec(memory_space=pltpu.VMEM)
    macs = 6 * GROUP * frames * span * 2 * PAIRS * HEAD
    operands = (queries, keys, values, grad_out, rel_bias)
    parts, bias = pl.pallas_call(
        functools.partial(kernel, n_dp, n_groups, frames),
        out_shape=(
            jax.ShapeDtypeStruct((4, frames, width), bf16),
            jax.ShapeDtypeStruct((PAIRS, GROUP, 16, 128), f32),
        ),
        in_specs=[hbm, hbm, hbm, hbm, hbm],
        out_specs=(anywhere, vmem),
        scratch_shapes=[
            pltpu.VMEM((4, frames, width), bf16),
            pltpu.VMEM(rel_bias.shape, f32),
            pltpu.VMEM((PAIRS, 2, own, LANES), bf16),
            pltpu.VMEM((PAIRS, 2, rows, LANES), bf16),
            pltpu.VMEM((HEADS, span), f32),
            pltpu.VMEM((PAIRS, 2 * frames, span), f32),
            pltpu.VMEM((PAIRS, 2 * frames, span), f32),
            pltpu.VMEM((PAIRS, LANES, rows), f32),
            pltpu.VMEM((PAIRS, LANES, rows), f32),
            pltpu.VMEM((2, 2 * frames, span), f32),
            pltpu.VMEM((2, 2 * frames, span), f32),
            pltpu.VMEM((2, 2 * frames, span), f32),
            pltpu.VMEM((2, 2 * frames, span), bf16),
            pltpu.VMEM((2, 2 * frames, span), bf16),
            pltpu.VMEM((2, LANES, 2 * frames), bf16),
            pltpu.VMEM((2, LANES, 2 * frames), bf16),
            pltpu.VMEM((PAIRS, 2, NB, 2, LANES, frames), bf16),
            pltpu.VMEM((PAIRS, 2, NB, 2, LANES, frames), bf16),
            pltpu.VMEM((PAIRS, GROUP, 4, frames, LANES), bf16),
            pltpu.VMEM((PAIRS, n_peer, 16, 128), f32),
            pltpu.VMEM((PAIRS, 16, 128), f32),
            dma((5,)),
            dma((1,)),
            dma((PAIRS, GROUP)),
            dma((PAIRS,)),
            dma((2,)),
            dma((PAIRS, 2)),
            dma((2,)),
            dma((PAIRS, 2, NB)),
            dma((1,)),
            dma((1,)),
            dma((1,)),
            dma((1,)),
            dma((PAIRS,)),
            dma((1,)),
            dma((PAIRS,)),
        ],
        compiler_params=pltpu.CompilerParams(
            collective_id=0, has_side_effects=True, vmem_limit_bytes=VMEM_LIMIT
        ),
        cost_estimate=pl.CostEstimate(
            flops=2 * macs, bytes_accessed=8 * frames * width * 2, transcendentals=own * span * 2 * PAIRS
        ),
    )(*(pltpu.with_memory_space_constraint(x, pltpu.HBM) for x in operands))
    return pl.pallas_call(
        finish,
        out_shape=(block, block, block, block, jax.ShapeDtypeStruct(rel_bias.shape, f32)),
        in_specs=[vmem, vmem],
        out_specs=(hbm, hbm, hbm, hbm, vmem),
        scratch_shapes=[dma((4,))],
        compiler_params=pltpu.CompilerParams(vmem_limit_bytes=VMEM_LIMIT),
        cost_estimate=pl.CostEstimate(
            flops=0, bytes_accessed=8 * frames * width * 2, transcendentals=0
        ),
    )(parts, bias)


def solution(mesh):
    placed = (
        P("dp", "ctx", None),
        P("dp", "ctx", None),
        P("dp", "ctx", None),
        P(),
        P("dp", "ctx", None),
    )
    return jax.shard_map(
        body,
        mesh=mesh,
        in_specs=placed,
        out_specs=(
            P("dp", "ctx", None),
            P("dp", "ctx", None),
            P("dp", "ctx", None),
            P("dp", "ctx", None),
            P(),
        ),
        check_vma=False,
    )
```

```python
import functools
import math

import jax
import jax.numpy as jnp
from jax import lax
from jax.experimental import pallas as pl
from jax.experimental.pallas import tpu as pltpu
from jax.sharding import PartitionSpec as P

HEADS = 16
HEAD = 64
NB = 3
GROUP = 4
PAIRS = HEADS // GROUP // 2
LANES = 2 * HEAD
EXCLUDED = -1e30
VMEM_LIMIT = 40 * 1024 * 1024
MESH = pl.DeviceIdType.MESH
K, V, Q, G = 0, 1, 2, 3
STRIP = 16
NT = (((1,), (1,)), ((), ()))


ORDER = (0, 3, 1, 2)
DONE = {0: ((0, 0),), 3: ((1, 2),), 1: ((0, 1),), 2: ((1, 0), (1, 1), (0, 2))}


def dot(a, b, dims=(((1,), (0,)), ((), ()))):
    return lax.dot_general(a, b, dims, preferred_element_type=jnp.float32)


def mirror_lanes(x):
    row = lax.broadcasted_iota(jnp.int32, (128, 128), 0)
    col = lax.broadcasted_iota(jnp.int32, (128, 128), 1)
    exchange = (row + col == 127).astype(jnp.float32)
    return jnp.dot(
        x, exchange, precision=lax.Precision.HIGHEST, preferred_element_type=jnp.float32
    )


def kernel(
    n_dp, n_groups, frames,
    q_hbm, k_hbm, v_hbm, g_hbm, rel_hbm,
    parts_out, bias_out,
    inbuf, rel_ref, qgbuf, kvbuf, rev_buf, bias_tab, bias_acc, gk_acc, gv_acc,
    score_buf, prob_buf, dprob_buf, ds_buf, w_buf, qt_buf, gt_buf, halo_out, halo_in, ostage, b1buf, sum_buf,
    loc_sem, a_send, kv_recv, qg_recv, h_send, h_recv, g_send, g_recv,
    o_send, o_recv, o_loc, b1_send, b1_recv, b2_send, b2_recv,
):
    span = (2 * NB + 1) * frames
    ctxw = NB * frames
    own = GROUP * frames
    score_scale = 1.0 / math.sqrt(HEAD)
    dp = lax.axis_index("dp")
    ctx = lax.axis_index("ctx")
    g = lax.div(ctx, GROUP)
    i = lax.rem(ctx, GROUP)
    n_peer = n_dp * n_groups
    slot = dp * n_groups + g
    has_lo = g > 0
    has_hi = g < n_groups - 1
    srcs = (k_hbm, v_hbm, q_hbm, g_hbm)
    accs = (gk_acc, gv_acc)

    def group_dev(j):
        return {"dp": dp, "ctx": g * GROUP + j}

    def side_dev(direction):
        return {"dp": dp, "ctx": ctx + (GROUP if direction else -GROUP)}

    def peer_dev(s):
        return {"dp": lax.div(s, n_groups), "ctx": lax.rem(s, n_groups) * GROUP + i}

    def tile(j, p):
        return j * PAIRS + p

    def pair_rows(half, p, j):
        if half == 0:
            return kvbuf.at[p, :, pl.ds(pl.multiple_of(ctxw + j * frames, frames), frames), :]
        return qgbuf.at[p, :, pl.ds(pl.multiple_of(j * frames, frames), frames), :]

    def load(arr, t):
        return pltpu.make_async_copy(
            srcs[arr].at[0, :, t * LANES : (t + 1) * LANES], inbuf.at[t, arr], loc_sem.at[0]
        )

    def place_own(half, p):
        pair_rows(half, p, i)[...] = inbuf[tile(i, p), 2 * half : 2 * half + 2]

    def remote(src, dst, send_sem, recv_sem, device):
        return pltpu.make_async_remote_copy(
            src_ref=src, dst_ref=dst, send_sem=send_sem, recv_sem=recv_sem,
            device_id=device, device_id_type=MESH,
        )

    def a_copy(half, p, j):
        recv = qg_recv.at[p] if half else kv_recv.at[p, i]
        return remote(
            inbuf.at[tile(j, p), pl.ds(2 * half, 2)], pair_rows(half, p, i),
            a_send.at[0], recv, group_dev(j),
        )

    def kv_arrival(p, j):
        block = kvbuf.at[p, :, pl.ds(pl.multiple_of(ctxw + j * frames, frames), frames), :]
        return remote(block, block, a_send.at[0], kv_recv.at[p, j], group_dev(j))

    def qg_arrival(p):
        blocks = qgbuf.at[p, :, pl.ds(0, own - frames), :]
        return remote(blocks, blocks, a_send.at[0], qg_recv.at[p], group_dev(i))

    def halo_copy(p, direction, j):
        src = pl.multiple_of(ctxw + j * frames, frames)
        place = j - 1 if direction else j
        dst = pl.multiple_of(place * frames + (0 if direction else ctxw + own), frames)
        return remote(
            kvbuf.at[p, :, pl.ds(src, frames), :],
            kvbuf.at[p, :, pl.ds(dst, frames), :],
            h_send.at[direction], h_recv.at[p, direction], side_dev(direction),
        )

    def halo_arrival(p, direction):
        blocks = kvbuf.at[p, :, pl.ds(0 if direction else ctxw + own, ctxw), :]
        return remote(
            blocks, blocks, h_send.at[direction], h_recv.at[p, direction], side_dev(direction)
        )

    def grad_copy(p, direction, blk):
        return remote(
            halo_out.at[p, direction, blk], halo_in.at[p, direction, blk],
            g_send.at[direction], g_recv.at[p, direction, blk], side_dev(direction),
        )

    def out_parts(half, p, j):
        return ostage.at[p, j, pl.ds(2 * half, 2)]

    def out_copy(half, p, j):
        return remote(
            out_parts(half, p, j), parts_out.at[tile(i, p), pl.ds(2 * half, 2)],
            o_send.at[0], o_recv.at[0], group_dev(j),
        )

    def send_out(half, p, j):
        @pl.when(j != i)
        def _():
            out_copy(half, p, j).start()

        @pl.when(j == i)
        def _():
            pltpu.make_async_copy(
                out_parts(half, p, j), parts_out.at[tile(i, p), pl.ds(2 * half, 2)], o_loc.at[0]
            ).start()

    def b1_copy(p, s):
        return remote(
            b1buf.at[p, slot], b1buf.at[p, slot], b1_send.at[0], b1_recv.at[p], peer_dev(s)
        )

    def b2_copy(p, j):
        return remote(sum_buf.at[p], bias_out.at[p, i], b2_send.at[0], b2_recv.at[p], group_dev(j))

    def others(fn):
        core = lax.rem(i, 2)
        far = 2 - 2 * lax.div(i, 2)
        fn(i + 1 - 2 * core)
        fn(far + core)
        fn(far + 1 - core)

    def all_peers(fn):
        def step(t, carry):
            fn(lax.rem(slot + t, n_peer))
            return carry

        lax.fori_loop(1, n_peer, step, 0)

    barrier = pltpu.get_barrier_semaphore()

    def greet(device):
        pl.semaphore_signal(barrier, inc=1, device_id=device, device_id_type=MESH)

    others(lambda j: greet(group_dev(j)))
    all_peers(lambda s: greet(peer_dev(s)))
    load_rel = pltpu.make_async_copy(rel_hbm, rel_ref, loc_sem.at[1])
    for t in range(GROUP * PAIRS):
        for arr in (K, V, Q, G):
            load(arr, t).start()
    load_rel.start()

    bias_acc[...] = jnp.zeros_like(bias_acc)
    gk_acc[...] = jnp.zeros_like(gk_acc)
    gv_acc[...] = jnp.zeros_like(gv_acc)
    edge_zero = jnp.zeros((PAIRS, 2, ctxw, LANES), jnp.bfloat16)
    edge_grad = jnp.zeros((PAIRS, NB, 2, LANES, frames), jnp.bfloat16)

    @pl.when(jnp.logical_not(has_lo))
    def _():
        kvbuf[:, :, :ctxw, :] = edge_zero
        halo_in[:, 1] = edge_grad

    @pl.when(jnp.logical_not(has_hi))
    def _():
        kvbuf[:, :, ctxw + own :, :] = edge_zero
        halo_in[:, 0] = edge_grad

    pl.semaphore_wait(barrier, GROUP - 1 + n_peer - 1)

    def send_inputs(p):
        for half in range(2):
            others(lambda j: a_copy(half, p, j).start())

    pltpu.make_async_copy(inbuf, inbuf, loc_sem.at[0]).wait()
    send_inputs(0)
    for p in range(PAIRS):
        for half in range(2):
            place_own(half, p)
    load_rel.wait()

    chunks = 2 * ctxw // 128
    for c in range(chunks):
        rev_buf[:, (chunks - 1 - c) * 128 : (chunks - c) * 128] = mirror_lanes(
            rel_ref[:, c * 128 : (c + 1) * 128]
        )
    last_lane = lax.broadcasted_iota(jnp.int32, (HEADS, 128), 1) == 127
    rev_buf[:, 2 * ctxw :] = jnp.where(
        last_lane, rel_ref[:, 2 * ctxw : 2 * ctxw + 1], jnp.float32(EXCLUDED)
    )
    for p in range(PAIRS):
        for h in range(2):
            row = rev_buf[pl.ds(i * (2 * PAIRS) + 2 * p + h, 1), :]
            table = jnp.broadcast_to(row, (frames, span))
            bias_tab[p, h * frames : (h + 1) * frames, :] = pltpu.roll(
                table, 1, 1, stride=1, stride_axis=0
            )
    def forward_halo(p):
        def forward(j):
            @pl.when(has_lo & (j < NB))
            def _():
                halo_copy(p, 0, j).start()

            @pl.when(has_hi & (j > 0))
            def _():
                halo_copy(p, 1, j).start()

        forward(i)

        def passed_on(j):
            kv_arrival(p, j).wait_recv()
            forward(j)

        others(passed_on)

    def wait_inputs(p):
        qg_arrival(p).wait_recv()

        @pl.when(has_lo)
        def _():
            halo_arrival(p, 1).wait_recv()

        @pl.when(has_hi)
        def _():
            halo_arrival(p, 0).wait_recv()

    low = lax.broadcasted_iota(jnp.int32, (frames, LANES), 1) < HEAD

    def stack_heads(x):
        zero = jnp.zeros_like(x)
        return jnp.concatenate([jnp.where(low, x, zero), jnp.where(low, zero, x)], axis=0)

    def merge_heads(x):
        return jnp.where(low, x[:frames], x[frames:])

    column = lax.broadcasted_iota(jnp.int32, (1, span), 1)

    top_half = lax.broadcasted_iota(jnp.int32, (LANES, frames), 0) < HEAD

    def stack_turned(x):
        turned = x.T
        zero = jnp.zeros_like(turned)
        return jnp.concatenate(
            [jnp.where(top_half, turned, zero), jnp.where(top_half, zero, turned)], axis=1
        ).astype(jnp.bfloat16)

    def softmax_part(n, p, b):
        own_rows = slice(b * frames, (b + 1) * frames)
        window = slice(b * frames, b * frames + span)
        key_row = column + ((g * GROUP - NB + b) * frames)
        exists = (key_row >= 0) & (key_row < n_groups * own)
        edge = jnp.where(exists, 0.0, EXCLUDED).astype(jnp.float32)
        kw = kvbuf[p, 0, window, :]
        vw = kvbuf[p, 1, window, :]
        q32 = qgbuf[p, 0, own_rows, :].astype(jnp.float32) * score_scale
        g32 = qgbuf[p, 1, own_rows, :].astype(jnp.float32)
        qs = stack_heads(q32).astype(jnp.bfloat16)
        gs32 = stack_heads(g32)
        gs = gs32.astype(jnp.bfloat16)
        qt_buf[n % 2] = stack_turned(q32)
        gt_buf[n % 2] = stack_turned(g32)
        m = n % 2
        score_buf[m] = dot(qs, kw, NT)
        dprob_buf[m] = dot(gs, vw, NT)
        for r in range(0, 2 * frames, STRIP):
            strip = slice(r, r + STRIP)
            scores = score_buf[m, strip, :] + bias_tab[p, strip, :] + edge
            top = jnp.max(scores, axis=1, keepdims=True)
            expd = jnp.exp(scores - top)
            total = jnp.sum(expd, axis=1, keepdims=True)
            probs = expd * (1.0 / total)
            prob_buf[m, strip, :] = probs
            w_buf[m, strip, :] = probs.astype(jnp.bfloat16)
        weights = w_buf[m]
        attended = merge_heads(dot(weights, vw)).astype(jnp.bfloat16)
        ostage[p, b, 0] = attended
        wide = attended.astype(jnp.float32)
        delta = jnp.sum(gs32 * jnp.concatenate([wide, wide], axis=0), axis=1, keepdims=True)
        for r in range(0, 2 * frames, STRIP):
            strip = slice(r, r + STRIP)
            dscore = prob_buf[m, strip, :] * (dprob_buf[m, strip, :] - delta[strip])
            ds_buf[m, strip, :] = dscore.astype(jnp.bfloat16)
            bias_acc[p, strip, :] += dscore

    def grad_part(n, p, b):
        window = slice(b * frames, b * frames + span)
        dscore_low = ds_buf[n % 2]
        grad_q = merge_heads(dot(dscore_low, kvbuf[p, 0, window, :])) * score_scale
        ostage[p, b, 1] = grad_q.astype(jnp.bfloat16)
        gk_acc[p, :, window] += dot(qt_buf[n % 2], dscore_low)
        gv_acc[p, :, window] += dot(gt_buf[n % 2], w_buf[n % 2])

    def send_grads(p, b):
        send_out(0, p, b)
        for direction, blk in DONE[b]:
            start = blk * frames + (ctxw + own if direction else 0)

            @pl.when(has_hi if direction else has_lo)
            def _():
                for a in range(2):
                    halo_out[p, direction, blk, a] = accs[a][p, :, start : start + frames].astype(
                        jnp.bfloat16
                    )
                grad_copy(p, direction, blk).start()

    def send_bias(p):
        sub = lax.broadcasted_iota(jnp.int32, (8, span), 0)
        b1buf[p, slot] = jnp.zeros((16, 128), jnp.float32)
        for h in range(2):
            part = bias_acc[p, h * frames : (h + 1) * frames, :]
            rows = frames
            while rows > 8:
                rows //= 2
                part = part[:rows] + pltpu.roll(part[rows:], span - rows, 1)
            for s in (4, 2, 1):
                part = jnp.where((sub & s) != 0, pltpu.roll(part, span - s, 1), part)
            diag = pltpu.roll(jnp.sum(part, axis=0, keepdims=True), span - 1, 1)
            for c in range(span // 128):
                n = h * (span // 128) + c
                b1buf[p, slot, n : n + 1, :] = diag[:, c * 128 : (c + 1) * 128]
        all_peers(lambda s: b1_copy(p, s).start())

    def sum_bias(p):
        others_part = b1buf.at[p, pl.ds(0, n_peer - 1)]
        remote(
            others_part, others_part, b1_send.at[0], b1_recv.at[p], group_dev(i)
        ).wait_recv()
        sum_buf[p] = lax.fori_loop(
            0, n_peer, lambda s, acc: acc + b1buf[p, s], jnp.zeros((16, 128), jnp.float32)
        )
        others(lambda j: b2_copy(p, j).start())
        bias_out[p, i] = sum_buf[p]

    def finish_grads(p):
        for j in (2, 0, 1, 3):
            if j < NB:
                @pl.when(has_lo)
                def _():
                    grad_copy(p, 1, j).wait_recv()
            if j > 0:
                @pl.when(has_hi)
                def _():
                    grad_copy(p, 0, j - 1).wait_recv()
            start = ctxw + j * frames
            for a in range(2):
                full = accs[a][p, :, start : start + frames]
                if j < NB:
                    full = full + halo_in[p, 1, j, a].astype(jnp.float32)
                if j > 0:
                    full = full + halo_in[p, 0, j - 1, a].astype(jnp.float32)
                ostage[p, j, 2 + a] = full.T.astype(jnp.bfloat16)
            send_out(1, p, j)

    units = [(p, b) for p in range(PAIRS) for b in ORDER]
    forward_halo(0)
    for p in range(1, PAIRS):
        send_inputs(p)
    for n, (p, b) in enumerate(units):
        if b == ORDER[0]:
            wait_inputs(p)
        softmax_part(n, p, b)
        if n > 0:
            grad_part(n - 1, *units[n - 1])
            send_grads(*units[n - 1])
        if b == ORDER[0]:
            if p + 1 < PAIRS:
                forward_halo(p + 1)
            if p > 0:
                send_bias(p - 1)
        if b == ORDER[2] and p > 0:
            sum_bias(p - 1)
            finish_grads(p - 1)
    grad_part(len(units) - 1, *units[-1])
    send_grads(*units[-1])
    send_bias(PAIRS - 1)
    finish_grads(PAIRS - 1)
    sum_bias(PAIRS - 1)

    def drain_send(ref, sem):
        remote(ref, ref, sem, sem, group_dev(i)).wait_send()

    def drain_recv(ref, sem):
        remote(ref, ref, sem, sem, group_dev(i)).wait_recv()

    for p in range(PAIRS):
        drain_recv(bias_out.at[p, pl.ds(0, GROUP - 1)], b2_recv.at[p])
    drain_recv(parts_out.at[pl.ds(0, (GROUP - 1) * PAIRS)], o_recv.at[0])
    own_part = parts_out.at[pl.ds(0, PAIRS)]
    pltpu.make_async_copy(own_part, own_part, o_loc.at[0]).wait()
    drain_send(parts_out.at[pl.ds(0, (GROUP - 1) * PAIRS)], o_send.at[0])
    drain_send(parts_out.at[pl.ds(0, (GROUP - 1) * PAIRS)], a_send.at[0])
    for direction, exists in ((0, has_lo), (1, has_hi)):
        @pl.when(exists)
        def _():
            drain_send(kvbuf.at[:, :, pl.ds(0, ctxw), :], h_send.at[direction])
            drain_send(halo_out.at[:, direction], g_send.at[direction])

    drain_send(b1buf.at[:, pl.ds(0, n_peer - 1)], b1_send.at[0])
    drain_send(bias_out.at[:, pl.ds(0, GROUP - 1)], b2_send.at[0])


def finish(parts, bias, att_out, gq_out, gk_out, gv_out, bias_out, sems):
    outs = (att_out, gq_out, gk_out, gv_out)
    leave = [
        pltpu.make_async_copy(
            parts.at[t, n], outs[n].at[0, :, t * LANES : (t + 1) * LANES], sems.at[n]
        )
        for t in range(GROUP * PAIRS)
        for n in range(4)
    ]
    for copy in leave:
        copy.start()
    chunks = bias_out.shape[1] // 128
    mirrored = mirror_lanes(bias[...].reshape(PAIRS * GROUP * 16, 128))
    for head in range(HEADS):
        dev, pair, odd = head // (2 * PAIRS), head // 2 % PAIRS, head % 2
        base = (pair * GROUP + dev) * 16 + odd * (chunks + 1)
        for c in range(chunks):
            place = (chunks - 1 - c) * 128
            bias_out[head : head + 1, place : place + 128] = mirrored[base + c : base + c + 1, :]
        bias_out[head : head + 1, chunks * 128 :] = mirrored[base + chunks : base + chunks + 1, :1]
    for n in range(4):
        pltpu.make_async_copy(outs[n], outs[n], sems.at[n]).wait()


def body(queries, keys, values, rel_bias, grad_out):
    rec_dev, frames, width = queries.shape
    n_dp = lax.axis_size("dp")
    n_groups = lax.axis_size("ctx") // GROUP
    n_peer = n_dp * n_groups
    span = (2 * NB + 1) * frames
    ctxw = NB * frames
    own = GROUP * frames
    rows = own + 2 * ctxw
    block = jax.ShapeDtypeStruct(queries.shape, jnp.bfloat16)
    bf16, f32 = jnp.bfloat16, jnp.float32
    dma = pltpu.SemaphoreType.DMA
    anywhere = pl.BlockSpec(memory_space=pl.ANY)
    hbm = pl.BlockSpec(memory_space=pltpu.HBM)
    vmem = pl.BlockSpec(memory_space=pltpu.VMEM)
    macs = 6 * GROUP * frames * span * 2 * PAIRS * HEAD
    operands = (queries, keys, values, grad_out, rel_bias)
    parts, bias = pl.pallas_call(
        functools.partial(kernel, n_dp, n_groups, frames),
        out_shape=(
            jax.ShapeDtypeStruct((GROUP * PAIRS, 4, frames, LANES), bf16),
            jax.ShapeDtypeStruct((PAIRS, GROUP, 16, 128), f32),
        ),
        in_specs=[hbm, hbm, hbm, hbm, hbm],
        out_specs=(anywhere, vmem),
        scratch_shapes=[
            pltpu.VMEM((GROUP * PAIRS, 4, frames, LANES), bf16),
            pltpu.VMEM(rel_bias.shape, f32),
            pltpu.VMEM((PAIRS, 2, own, LANES), bf16),
            pltpu.VMEM((PAIRS, 2, rows, LANES), bf16),
            pltpu.VMEM((HEADS, span), f32),
            pltpu.VMEM((PAIRS, 2 * frames, span), f32),
            pltpu.VMEM((PAIRS, 2 * frames, span), f32),
            pltpu.VMEM((PAIRS, LANES, rows), f32),
            pltpu.VMEM((PAIRS, LANES, rows), f32),
            pltpu.VMEM((2, 2 * frames, span), f32),
            pltpu.VMEM((2, 2 * frames, span), f32),
            pltpu.VMEM((2, 2 * frames, span), f32),
            pltpu.VMEM((2, 2 * frames, span), bf16),
            pltpu.VMEM((2, 2 * frames, span), bf16),
            pltpu.VMEM((2, LANES, 2 * frames), bf16),
            pltpu.VMEM((2, LANES, 2 * frames), bf16),
            pltpu.VMEM((PAIRS, 2, NB, 2, LANES, frames), bf16),
            pltpu.VMEM((PAIRS, 2, NB, 2, LANES, frames), bf16),
            pltpu.VMEM((PAIRS, GROUP, 4, frames, LANES), bf16),
            pltpu.VMEM((PAIRS, n_peer, 16, 128), f32),
            pltpu.VMEM((PAIRS, 16, 128), f32),
            dma((2,)),
            dma((1,)),
            dma((PAIRS, GROUP)),
            dma((PAIRS,)),
            dma((2,)),
            dma((PAIRS, 2)),
            dma((2,)),
            dma((PAIRS, 2, NB)),
            dma((1,)),
            dma((1,)),
            dma((1,)),
            dma((1,)),
            dma((PAIRS,)),
            dma((1,)),
            dma((PAIRS,)),
        ],
        compiler_params=pltpu.CompilerParams(
            collective_id=0, has_side_effects=True, vmem_limit_bytes=VMEM_LIMIT
        ),
        cost_estimate=pl.CostEstimate(
            flops=2 * macs, bytes_accessed=8 * frames * width * 2, transcendentals=own * span * 2 * PAIRS
        ),
    )(*(pltpu.with_memory_space_constraint(x, pltpu.HBM) for x in operands))
    return pl.pallas_call(
        finish,
        out_shape=(block, block, block, block, jax.ShapeDtypeStruct(rel_bias.shape, f32)),
        in_specs=[vmem, vmem],
        out_specs=(hbm, hbm, hbm, hbm, vmem),
        scratch_shapes=[dma((4,))],
        compiler_params=pltpu.CompilerParams(vmem_limit_bytes=VMEM_LIMIT),
        cost_estimate=pl.CostEstimate(
            flops=0, bytes_accessed=8 * frames * width * 2, transcendentals=0
        ),
    )(parts, bias)


def solution(mesh):
    placed = (
        P("dp", "ctx", None),
        P("dp", "ctx", None),
        P("dp", "ctx", None),
        P(),
        P("dp", "ctx", None),
    )
    return jax.shard_map(
        body,
        mesh=mesh,
        in_specs=placed,
        out_specs=(
            P("dp", "ctx", None),
            P("dp", "ctx", None),
            P("dp", "ctx", None),
            P("dp", "ctx", None),
            P(),
        ),
        check_vma=False,
    )
```

```python
import functools
import math

import jax
import jax.numpy as jnp
from jax import lax
from jax.experimental import pallas as pl
from jax.experimental.pallas import tpu as pltpu
from jax.sharding import PartitionSpec as P

HEADS = 16
HEAD = 64
NB = 3
GROUP = 4
PAIRS = HEADS // GROUP // 2
LANES = 2 * HEAD
EXCLUDED = -1e30
VMEM_LIMIT = 40 * 1024 * 1024
MESH = pl.DeviceIdType.MESH
K, V, Q, G = 0, 1, 2, 3
STRIP = 16
NT = (((1,), (1,)), ((), ()))


ORDER = (0, 3, 1, 2)
DONE = {0: ((0, 0),), 3: ((1, 2),), 1: ((0, 1),), 2: ((1, 0), (1, 1), (0, 2))}


def dot(a, b, dims=(((1,), (0,)), ((), ()))):
    return lax.dot_general(a, b, dims, preferred_element_type=jnp.float32)


def mirror_lanes(x):
    row = lax.broadcasted_iota(jnp.int32, (128, 128), 0)
    col = lax.broadcasted_iota(jnp.int32, (128, 128), 1)
    exchange = (row + col == 127).astype(jnp.float32)
    return jnp.dot(
        x, exchange, precision=lax.Precision.HIGHEST, preferred_element_type=jnp.float32
    )


def kernel(
    n_dp, n_groups, frames,
    q_hbm, k_hbm, v_hbm, g_hbm, rel_hbm,
    parts_out, bias_out,
    inbuf, rel_ref, qgbuf, kvbuf, rev_buf, bias_tab, bias_acc, gk_acc, gv_acc,
    score_buf, prob_buf, dprob_buf, ds_buf, w_buf, qt_buf, gt_buf, halo_out, halo_in, ostage, b1buf, sum_buf,
    loc_sem, a_send, kv_recv, qg_recv, h_send, h_recv, g_send, g_recv,
    o_send, o_recv, o_loc, b1_send, b1_recv, b2_send, b2_recv,
):
    span = (2 * NB + 1) * frames
    ctxw = NB * frames
    own = GROUP * frames
    score_scale = 1.0 / math.sqrt(HEAD)
    dp = lax.axis_index("dp")
    ctx = lax.axis_index("ctx")
    g = lax.div(ctx, GROUP)
    i = lax.rem(ctx, GROUP)
    n_peer = n_dp * n_groups
    slot = dp * n_groups + g
    has_lo = g > 0
    has_hi = g < n_groups - 1
    srcs = (k_hbm, v_hbm, q_hbm, g_hbm)
    accs = (gk_acc, gv_acc)

    def group_dev(j):
        return {"dp": dp, "ctx": g * GROUP + j}

    def side_dev(direction):
        return {"dp": dp, "ctx": ctx + (GROUP if direction else -GROUP)}

    def peer_dev(s):
        return {"dp": lax.div(s, n_groups), "ctx": lax.rem(s, n_groups) * GROUP + i}

    def tile(j, p):
        return j * PAIRS + p

    def pair_rows(half, p, j):
        if half == 0:
            return kvbuf.at[p, :, pl.ds(pl.multiple_of(ctxw + j * frames, frames), frames), :]
        return qgbuf.at[p, :, pl.ds(pl.multiple_of(j * frames, frames), frames), :]

    def load(arr, t):
        return pltpu.make_async_copy(
            srcs[arr].at[0, :, t * LANES : (t + 1) * LANES], inbuf.at[t, arr], loc_sem.at[0]
        )

    def place_own(half, p):
        pair_rows(half, p, i)[...] = inbuf[tile(i, p), 2 * half : 2 * half + 2]

    def remote(src, dst, send_sem, recv_sem, device):
        return pltpu.make_async_remote_copy(
            src_ref=src, dst_ref=dst, send_sem=send_sem, recv_sem=recv_sem,
            device_id=device, device_id_type=MESH,
        )

    def a_copy(half, p, j):
        recv = qg_recv.at[p] if half else kv_recv.at[p, i]
        return remote(
            inbuf.at[tile(j, p), pl.ds(2 * half, 2)], pair_rows(half, p, i),
            a_send.at[0], recv, group_dev(j),
        )

    def kv_arrival(p, j):
        block = kvbuf.at[p, :, pl.ds(pl.multiple_of(ctxw + j * frames, frames), frames), :]
        return remote(block, block, a_send.at[0], kv_recv.at[p, j], group_dev(j))

    def qg_arrival(p):
        blocks = qgbuf.at[p, :, pl.ds(0, own - frames), :]
        return remote(blocks, blocks, a_send.at[0], qg_recv.at[p], group_dev(i))

    def halo_copy(p, direction, j):
        src = pl.multiple_of(ctxw + j * frames, frames)
        place = j - 1 if direction else j
        dst = pl.multiple_of(place * frames + (0 if direction else ctxw + own), frames)
        return remote(
            kvbuf.at[p, :, pl.ds(src, frames), :],
            kvbuf.at[p, :, pl.ds(dst, frames), :],
            h_send.at[direction], h_recv.at[p, direction], side_dev(direction),
        )

    def halo_arrival(p, direction):
        blocks = kvbuf.at[p, :, pl.ds(0 if direction else ctxw + own, ctxw), :]
        return remote(
            blocks, blocks, h_send.at[direction], h_recv.at[p, direction], side_dev(direction)
        )

    def grad_copy(p, direction, blk):
        return remote(
            halo_out.at[p, direction, blk], halo_in.at[p, direction, blk],
            g_send.at[direction], g_recv.at[p, direction, blk], side_dev(direction),
        )

    def out_parts(half, p, j):
        return ostage.at[p, j, pl.ds(2 * half, 2)]

    def out_copy(half, p, j):
        return remote(
            out_parts(half, p, j), parts_out.at[tile(i, p), pl.ds(2 * half, 2)],
            o_send.at[0], o_recv.at[0], group_dev(j),
        )

    def send_out(half, p, j):
        @pl.when(j != i)
        def _():
            out_copy(half, p, j).start()

        @pl.when(j == i)
        def _():
            pltpu.make_async_copy(
                out_parts(half, p, j), parts_out.at[tile(i, p), pl.ds(2 * half, 2)], o_loc.at[0]
            ).start()

    def b1_copy(p, s):
        return remote(
            b1buf.at[p, slot], b1buf.at[p, slot], b1_send.at[0], b1_recv.at[p], peer_dev(s)
        )

    def b2_copy(p, j):
        return remote(sum_buf.at[p], bias_out.at[p, i], b2_send.at[0], b2_recv.at[p], group_dev(j))

    def others(fn):
        core = lax.rem(i, 2)
        far = 2 - 2 * lax.div(i, 2)
        fn(i + 1 - 2 * core)
        fn(far + core)
        fn(far + 1 - core)

    def all_peers(fn):
        def step(t, carry):
            fn(lax.rem(slot + t, n_peer))
            return carry

        lax.fori_loop(1, n_peer, step, 0)

    barrier = pltpu.get_barrier_semaphore()

    def greet(device):
        pl.semaphore_signal(barrier, inc=1, device_id=device, device_id_type=MESH)

    others(lambda j: greet(group_dev(j)))
    all_peers(lambda s: greet(peer_dev(s)))
    load_rel = pltpu.make_async_copy(rel_hbm, rel_ref, loc_sem.at[1])
    for t in range(GROUP * PAIRS):
        for arr in (K, V, Q, G):
            load(arr, t).start()
    load_rel.start()

    bias_acc[...] = jnp.zeros_like(bias_acc)
    gk_acc[...] = jnp.zeros_like(gk_acc)
    gv_acc[...] = jnp.zeros_like(gv_acc)
    edge_zero = jnp.zeros((PAIRS, 2, ctxw, LANES), jnp.bfloat16)
    edge_grad = jnp.zeros((PAIRS, NB, 2, LANES, frames), jnp.bfloat16)

    @pl.when(jnp.logical_not(has_lo))
    def _():
        kvbuf[:, :, :ctxw, :] = edge_zero
        halo_in[:, 1] = edge_grad

    @pl.when(jnp.logical_not(has_hi))
    def _():
        kvbuf[:, :, ctxw + own :, :] = edge_zero
        halo_in[:, 0] = edge_grad

    pl.semaphore_wait(barrier, GROUP - 1 + n_peer - 1)

    def send_inputs(half, p):
        others(lambda j: a_copy(half, p, j).start())

    pltpu.make_async_copy(inbuf, inbuf, loc_sem.at[0]).wait()
    for p in range(PAIRS):
        send_inputs(0, p)
    for p in range(PAIRS):
        for half in range(2):
            place_own(half, p)
    load_rel.wait()

    chunks = 2 * ctxw // 128
    for c in range(chunks):
        rev_buf[:, (chunks - 1 - c) * 128 : (chunks - c) * 128] = mirror_lanes(
            rel_ref[:, c * 128 : (c + 1) * 128]
        )
    last_lane = lax.broadcasted_iota(jnp.int32, (HEADS, 128), 1) == 127
    rev_buf[:, 2 * ctxw :] = jnp.where(
        last_lane, rel_ref[:, 2 * ctxw : 2 * ctxw + 1], jnp.float32(EXCLUDED)
    )
    for p in range(PAIRS):
        for h in range(2):
            row = rev_buf[pl.ds(i * (2 * PAIRS) + 2 * p + h, 1), :]
            table = jnp.broadcast_to(row, (frames, span))
            bias_tab[p, h * frames : (h + 1) * frames, :] = pltpu.roll(
                table, 1, 1, stride=1, stride_axis=0
            )
    def forward_halo(p):
        def forward(j):
            @pl.when(has_lo & (j < NB))
            def _():
                halo_copy(p, 0, j).start()

            @pl.when(has_hi & (j > 0))
            def _():
                halo_copy(p, 1, j).start()

        forward(i)

        def passed_on(j):
            kv_arrival(p, j).wait_recv()
            forward(j)

        others(passed_on)

    def wait_inputs(p):
        qg_arrival(p).wait_recv()

        @pl.when(has_lo)
        def _():
            halo_arrival(p, 1).wait_recv()

        @pl.when(has_hi)
        def _():
            halo_arrival(p, 0).wait_recv()

    low = lax.broadcasted_iota(jnp.int32, (frames, LANES), 1) < HEAD

    def stack_heads(x):
        zero = jnp.zeros_like(x)
        return jnp.concatenate([jnp.where(low, x, zero), jnp.where(low, zero, x)], axis=0)

    def merge_heads(x):
        return jnp.where(low, x[:frames], x[frames:])

    column = lax.broadcasted_iota(jnp.int32, (1, span), 1)

    top_half = lax.broadcasted_iota(jnp.int32, (LANES, frames), 0) < HEAD

    def stack_turned(x):
        turned = x.T
        zero = jnp.zeros_like(turned)
        return jnp.concatenate(
            [jnp.where(top_half, turned, zero), jnp.where(top_half, zero, turned)], axis=1
        ).astype(jnp.bfloat16)

    def softmax_part(n, p, b):
        own_rows = slice(b * frames, (b + 1) * frames)
        window = slice(b * frames, b * frames + span)
        key_row = column + ((g * GROUP - NB + b) * frames)
        exists = (key_row >= 0) & (key_row < n_groups * own)
        edge = jnp.where(exists, 0.0, EXCLUDED).astype(jnp.float32)
        kw = kvbuf[p, 0, window, :]
        vw = kvbuf[p, 1, window, :]
        q32 = qgbuf[p, 0, own_rows, :].astype(jnp.float32) * score_scale
        g32 = qgbuf[p, 1, own_rows, :].astype(jnp.float32)
        qs = stack_heads(q32).astype(jnp.bfloat16)
        gs32 = stack_heads(g32)
        gs = gs32.astype(jnp.bfloat16)
        qt_buf[n % 2] = stack_turned(q32)
        gt_buf[n % 2] = stack_turned(g32)
        m = n % 2
        score_buf[m] = dot(qs, kw, NT)
        dprob_buf[m] = dot(gs, vw, NT)
        for r in range(0, 2 * frames, STRIP):
            strip = slice(r, r + STRIP)
            scores = score_buf[m, strip, :] + bias_tab[p, strip, :] + edge
            top = jnp.max(scores, axis=1, keepdims=True)
            expd = jnp.exp(scores - top)
            total = jnp.sum(expd, axis=1, keepdims=True)
            probs = expd * (1.0 / total)
            prob_buf[m, strip, :] = probs
            w_buf[m, strip, :] = probs.astype(jnp.bfloat16)
        weights = w_buf[m]
        attended = merge_heads(dot(weights, vw)).astype(jnp.bfloat16)
        ostage[p, b, 0] = attended
        wide = attended.astype(jnp.float32)
        delta = jnp.sum(gs32 * jnp.concatenate([wide, wide], axis=0), axis=1, keepdims=True)
        for r in range(0, 2 * frames, STRIP):
            strip = slice(r, r + STRIP)
            dscore = prob_buf[m, strip, :] * (dprob_buf[m, strip, :] - delta[strip])
            ds_buf[m, strip, :] = dscore.astype(jnp.bfloat16)
            bias_acc[p, strip, :] += dscore

    def grad_part(n, p, b):
        window = slice(b * frames, b * frames + span)
        dscore_low = ds_buf[n % 2]
        grad_q = merge_heads(dot(dscore_low, kvbuf[p, 0, window, :])) * score_scale
        ostage[p, b, 1] = grad_q.astype(jnp.bfloat16)
        gk_acc[p, :, window] += dot(qt_buf[n % 2], dscore_low)
        gv_acc[p, :, window] += dot(gt_buf[n % 2], w_buf[n % 2])

    def send_grads(p, b):
        send_out(0, p, b)
        for direction, blk in DONE[b]:
            start = blk * frames + (ctxw + own if direction else 0)

            @pl.when(has_hi if direction else has_lo)
            def _():
                for a in range(2):
                    halo_out[p, direction, blk, a] = accs[a][p, :, start : start + frames].astype(
                        jnp.bfloat16
                    )
                grad_copy(p, direction, blk).start()

    def send_bias(p):
        sub = lax.broadcasted_iota(jnp.int32, (8, span), 0)
        b1buf[p, slot] = jnp.zeros((16, 128), jnp.float32)
        for h in range(2):
            part = bias_acc[p, h * frames : (h + 1) * frames, :]
            rows = frames
            while rows > 8:
                rows //= 2
                part = part[:rows] + pltpu.roll(part[rows:], span - rows, 1)
            for s in (4, 2, 1):
                part = jnp.where((sub & s) != 0, pltpu.roll(part, span - s, 1), part)
            diag = pltpu.roll(jnp.sum(part, axis=0, keepdims=True), span - 1, 1)
            for c in range(span // 128):
                n = h * (span // 128) + c
                b1buf[p, slot, n : n + 1, :] = diag[:, c * 128 : (c + 1) * 128]
        all_peers(lambda s: b1_copy(p, s).start())

    def sum_bias(p):
        others_part = b1buf.at[p, pl.ds(0, n_peer - 1)]
        remote(
            others_part, others_part, b1_send.at[0], b1_recv.at[p], group_dev(i)
        ).wait_recv()
        sum_buf[p] = lax.fori_loop(
            0, n_peer, lambda s, acc: acc + b1buf[p, s], jnp.zeros((16, 128), jnp.float32)
        )
        others(lambda j: b2_copy(p, j).start())
        bias_out[p, i] = sum_buf[p]

    def finish_grads(p):
        for j in (2, 0, 1, 3):
            if j < NB:
                @pl.when(has_lo)
                def _():
                    grad_copy(p, 1, j).wait_recv()
            if j > 0:
                @pl.when(has_hi)
                def _():
                    grad_copy(p, 0, j - 1).wait_recv()
            start = ctxw + j * frames
            for a in range(2):
                full = accs[a][p, :, start : start + frames]
                if j < NB:
                    full = full + halo_in[p, 1, j, a].astype(jnp.float32)
                if j > 0:
                    full = full + halo_in[p, 0, j - 1, a].astype(jnp.float32)
                ostage[p, j, 2 + a] = full.T.astype(jnp.bfloat16)
            send_out(1, p, j)

    units = [(p, b) for p in range(PAIRS) for b in ORDER]
    for p in range(PAIRS):
        forward_halo(p)
        send_inputs(1, p)
    for n, (p, b) in enumerate(units):
        if b == ORDER[0]:
            wait_inputs(p)
        softmax_part(n, p, b)
        if n > 0:
            grad_part(n - 1, *units[n - 1])
            send_grads(*units[n - 1])
        if b == ORDER[0] and p > 0:
            send_bias(p - 1)
        if b == ORDER[2] and p > 0:
            sum_bias(p - 1)
            finish_grads(p - 1)
    grad_part(len(units) - 1, *units[-1])
    send_grads(*units[-1])
    send_bias(PAIRS - 1)
    finish_grads(PAIRS - 1)
    sum_bias(PAIRS - 1)

    def drain_send(ref, sem):
        remote(ref, ref, sem, sem, group_dev(i)).wait_send()

    def drain_recv(ref, sem):
        remote(ref, ref, sem, sem, group_dev(i)).wait_recv()

    for p in range(PAIRS):
        drain_recv(bias_out.at[p, pl.ds(0, GROUP - 1)], b2_recv.at[p])
    drain_recv(parts_out.at[pl.ds(0, (GROUP - 1) * PAIRS)], o_recv.at[0])
    own_part = parts_out.at[pl.ds(0, PAIRS)]
    pltpu.make_async_copy(own_part, own_part, o_loc.at[0]).wait()
    drain_send(parts_out.at[pl.ds(0, (GROUP - 1) * PAIRS)], o_send.at[0])
    drain_send(parts_out.at[pl.ds(0, (GROUP - 1) * PAIRS)], a_send.at[0])
    for direction, exists in ((0, has_lo), (1, has_hi)):
        @pl.when(exists)
        def _():
            drain_send(kvbuf.at[:, :, pl.ds(0, ctxw), :], h_send.at[direction])
            drain_send(halo_out.at[:, direction], g_send.at[direction])

    drain_send(b1buf.at[:, pl.ds(0, n_peer - 1)], b1_send.at[0])
    drain_send(bias_out.at[:, pl.ds(0, GROUP - 1)], b2_send.at[0])


def finish(parts, bias, att_out, gq_out, gk_out, gv_out, bias_out, sems):
    outs = (att_out, gq_out, gk_out, gv_out)
    leave = [
        pltpu.make_async_copy(
            parts.at[t, n], outs[n].at[0, :, t * LANES : (t + 1) * LANES], sems.at[n]
        )
        for t in range(GROUP * PAIRS)
        for n in range(4)
    ]
    for copy in leave:
        copy.start()
    chunks = bias_out.shape[1] // 128
    mirrored = mirror_lanes(bias[...].reshape(PAIRS * GROUP * 16, 128))
    for head in range(HEADS):
        dev, pair, odd = head // (2 * PAIRS), head // 2 % PAIRS, head % 2
        base = (pair * GROUP + dev) * 16 + odd * (chunks + 1)
        for c in range(chunks):
            place = (chunks - 1 - c) * 128
            bias_out[head : head + 1, place : place + 128] = mirrored[base + c : base + c + 1, :]
        bias_out[head : head + 1, chunks * 128 :] = mirrored[base + chunks : base + chunks + 1, :1]
    for n in range(4):
        pltpu.make_async_copy(outs[n], outs[n], sems.at[n]).wait()


def body(queries, keys, values, rel_bias, grad_out):
    rec_dev, frames, width = queries.shape
    n_dp = lax.axis_size("dp")
    n_groups = lax.axis_size("ctx") // GROUP
    n_peer = n_dp * n_groups
    span = (2 * NB + 1) * frames
    ctxw = NB * frames
    own = GROUP * frames
    rows = own + 2 * ctxw
    block = jax.ShapeDtypeStruct(queries.shape, jnp.bfloat16)
    bf16, f32 = jnp.bfloat16, jnp.float32
    dma = pltpu.SemaphoreType.DMA
    anywhere = pl.BlockSpec(memory_space=pl.ANY)
    hbm = pl.BlockSpec(memory_space=pltpu.HBM)
    vmem = pl.BlockSpec(memory_space=pltpu.VMEM)
    macs = 6 * GROUP * frames * span * 2 * PAIRS * HEAD
    operands = (queries, keys, values, grad_out, rel_bias)
    parts, bias = pl.pallas_call(
        functools.partial(kernel, n_dp, n_groups, frames),
        out_shape=(
            jax.ShapeDtypeStruct((GROUP * PAIRS, 4, frames, LANES), bf16),
            jax.ShapeDtypeStruct((PAIRS, GROUP, 16, 128), f32),
        ),
        in_specs=[hbm, hbm, hbm, hbm, hbm],
        out_specs=(anywhere, vmem),
        scratch_shapes=[
            pltpu.VMEM((GROUP * PAIRS, 4, frames, LANES), bf16),
            pltpu.VMEM(rel_bias.shape, f32),
            pltpu.VMEM((PAIRS, 2, own, LANES), bf16),
            pltpu.VMEM((PAIRS, 2, rows, LANES), bf16),
            pltpu.VMEM((HEADS, span), f32),
            pltpu.VMEM((PAIRS, 2 * frames, span), f32),
            pltpu.VMEM((PAIRS, 2 * frames, span), f32),
            pltpu.VMEM((PAIRS, LANES, rows), f32),
            pltpu.VMEM((PAIRS, LANES, rows), f32),
            pltpu.VMEM((2, 2 * frames, span), f32),
            pltpu.VMEM((2, 2 * frames, span), f32),
            pltpu.VMEM((2, 2 * frames, span), f32),
            pltpu.VMEM((2, 2 * frames, span), bf16),
            pltpu.VMEM((2, 2 * frames, span), bf16),
            pltpu.VMEM((2, LANES, 2 * frames), bf16),
            pltpu.VMEM((2, LANES, 2 * frames), bf16),
            pltpu.VMEM((PAIRS, 2, NB, 2, LANES, frames), bf16),
            pltpu.VMEM((PAIRS, 2, NB, 2, LANES, frames), bf16),
            pltpu.VMEM((PAIRS, GROUP, 4, frames, LANES), bf16),
            pltpu.VMEM((PAIRS, n_peer, 16, 128), f32),
            pltpu.VMEM((PAIRS, 16, 128), f32),
            dma((2,)),
            dma((1,)),
            dma((PAIRS, GROUP)),
            dma((PAIRS,)),
            dma((2,)),
            dma((PAIRS, 2)),
            dma((2,)),
            dma((PAIRS, 2, NB)),
            dma((1,)),
            dma((1,)),
            dma((1,)),
            dma((1,)),
            dma((PAIRS,)),
            dma((1,)),
            dma((PAIRS,)),
        ],
        compiler_params=pltpu.CompilerParams(
            collective_id=0, has_side_effects=True, vmem_limit_bytes=VMEM_LIMIT
        ),
        cost_estimate=pl.CostEstimate(
            flops=2 * macs, bytes_accessed=8 * frames * width * 2, transcendentals=own * span * 2 * PAIRS
        ),
    )(*(pltpu.with_memory_space_constraint(x, pltpu.HBM) for x in operands))
    return pl.pallas_call(
        finish,
        out_shape=(block, block, block, block, jax.ShapeDtypeStruct(rel_bias.shape, f32)),
        in_specs=[vmem, vmem],
        out_specs=(hbm, hbm, hbm, hbm, vmem),
        scratch_shapes=[dma((4,))],
        compiler_params=pltpu.CompilerParams(vmem_limit_bytes=VMEM_LIMIT),
        cost_estimate=pl.CostEstimate(
            flops=0, bytes_accessed=8 * frames * width * 2, transcendentals=0
        ),
    )(parts, bias)


def solution(mesh):
    placed = (
        P("dp", "ctx", None),
        P("dp", "ctx", None),
        P("dp", "ctx", None),
        P(),
        P("dp", "ctx", None),
    )
    return jax.shard_map(
        body,
        mesh=mesh,
        in_specs=placed,
        out_specs=(
            P("dp", "ctx", None),
            P("dp", "ctx", None),
            P("dp", "ctx", None),
            P("dp", "ctx", None),
            P(),
        ),
        check_vma=False,
    )
```
